256 devices in a mesh: tile: 8 (over y, core), acq: 32 (over x, z).
Axes of the slice: x: 4, y: 4, z: 8, core: 2. Of those that a mesh axis runs over, the one named last changes fastest.
Arguments:
- complex_stack: float32 [128, 2, 1024, 512], P('acq', None, 'tile'), may hold values from -3 to 3, as said below
- pair_list: int32 [256, 2], P('acq'), may hold values from -1 to 127, as said below
- stack_order: int32 [128], replicated, may hold values from 0 to 127, as said below
- references: int32 [4], replicated, may hold values from 0 to 127, as said below
Outputs:
- series: float32 [131072, 128], P(('tile', 'acq'))
- coherence: float32 [256, 256, 512], P('acq', 'tile')
The draws below stay inside these ranges and needn't reach their ends.
Inputs may be any that keep to these rules, and one draw needn't show every extreme that they name: `complex_stack`: real and imaginary parts of complex values whose magnitude lies in 0.3 to 3 and whose phase lies in -pi/6 to pi/6. `pair_list`: rows p * 8 to p * 8 + 7 belong to index p of acq; each live row names a secondary stored on that index and a reference number; the live rows of a block come first and no (reference number, secondary) occurs twice; empty rows hold -1 in both columns; every block has one live row or more and some block is all live. `stack_order`: A permutation of the acquisition numbers. `references`: distinct acquisition numbers; acquisitions 0 and 127 are among them.
All inputs are finite; a program needn't handle non-finite values.
Results may differ from the reference program's by a relative error of at most 0.0003.
Values sent between devices are 32-bit elements; how exact they have to be, the bound alone decides.
A program may use at most 64 MiB of HBM per device.

```python
import jax
import jax.numpy as jnp
from jax import lax

NREF = 4
LOOKS = 4
A_DEV = 4
COLS = 512
CAP = 8
NACQ = 128
NPAIR = 256
ROWS = 1024
NPIX = 131072


def draw_layout(key):
    keys = jax.random.split(key, 7)
    order = jax.random.permutation(keys[0], NACQ).astype(jnp.int32)
    others = 1 + jax.random.permutation(keys[1], NACQ - 2)[:NREF - 2].astype(jnp.int32)
    ends = jnp.array([0, NACQ - 1], dtype=jnp.int32)
    gathered = jnp.concatenate([ends, others]).astype(jnp.int32)
    chosen = gathered[jax.random.permutation(keys[6], NREF)].astype(jnp.int32)
    devices = NACQ // A_DEV
    heavy = jax.random.randint(keys[2], (devices,), 0, 8) == 0
    forced = jax.random.randint(keys[3], (), 0, devices)
    base = jax.random.randint(keys[4], (devices,), 1, 4)
    device_ids = jnp.arange(devices, dtype=jnp.int32)
    counts = jnp.where(heavy | (device_ids == forced), CAP, base)
    combos = NREF * A_DEV
    scores = jax.random.randint(keys[5], (devices, combos), 0, 1 << 20) * combos + jnp.arange(combos, dtype=jnp.int32)[None, :]
    picked = jnp.argsort(scores, axis=1, stable=True)[:, :CAP].astype(jnp.int32)
    kinds = picked // A_DEV
    local_slot = picked % A_DEV
    seconds = order[device_ids[:, None] * A_DEV + local_slot]
    living = jnp.arange(CAP, dtype=jnp.int32)[None, :] < counts[:, None]
    pairs = jnp.stack([jnp.where(living, kinds, -1), jnp.where(living, seconds, -1)], axis=-1)
    return (pairs.reshape(devices * CAP, 2).astype(jnp.int32), order, chosen)


def draw_pair_list(key, part):
    return draw_layout(key)[0]


def draw_stack_order(key, part):
    return draw_layout(key)[1]


def draw_references(key, part):
    return draw_layout(key)[2]


def draw_complex_stack(key, part):
    key = jax.random.fold_in(key, 7)
    keys = jax.random.split(key, 3)
    grid_shape = (NACQ, ROWS, COLS)
    magnitude = 0.3 * jnp.exp(jnp.log(10.0) * jax.random.uniform(keys[0], grid_shape))
    angles = jax.random.uniform(keys[2], grid_shape, minval=-jnp.pi / 6, maxval=jnp.pi / 6)
    return jnp.stack([magnitude * jnp.cos(angles), magnitude * jnp.sin(angles)], axis=1).astype(jnp.float32)


def setup_inputs(seed: int = 0) -> dict:
    arg_keys = jax.random.split(jax.random.key(seed), 5)
    return {
        "complex_stack": draw_complex_stack(jax.random.fold_in(arg_keys[4], 71), 0),
        "pair_list": draw_pair_list(jax.random.fold_in(arg_keys[4], 71), 0),
        "stack_order": draw_stack_order(jax.random.fold_in(arg_keys[4], 71), 0),
        "references": draw_references(jax.random.fold_in(arg_keys[4], 71), 0),
    }


def window_sum(padded):
    inner_rows = padded.shape[-2] - 2
    row_total = padded[..., 0:inner_rows, :] + padded[..., 1:inner_rows + 1, :] + padded[..., 2:inner_rows + 2, :]
    columns = row_total.shape[-1]
    spread = jnp.pad(row_total, [(0, 0)] * (row_total.ndim - 1) + [(2, 2)])
    return spread[..., 0:columns] + spread[..., 1:columns + 1] + spread[..., 2:columns + 2] + spread[..., 3:columns + 3] + spread[..., 4:columns + 4]

def multilook(values):
    return values.reshape(values.shape[0] // LOOKS, LOOKS, values.shape[1]).sum(axis=1)

def reference(complex_stack, pair_list, stack_order, references):
    numbers = jnp.arange(NACQ, dtype=jnp.int32)
    inverse = jnp.zeros((NACQ,), jnp.int32).at[stack_order].set(numbers)
    kinds = pair_list[:, 0]
    living = kinds >= 0
    ref_acq = references[jnp.maximum(kinds, 0)]
    sec_acq = jnp.maximum(pair_list[:, 1], 0)

    def per_pair(slots):
        primary = complex_stack[slots[0]]
        second = complex_stack[slots[1]]
        first_real, first_imag = (primary[0], primary[1])
        second_real, second_imag = (second[0], second[1])
        look_real = multilook(first_real * second_real + first_imag * second_imag)
        look_imag = multilook(first_imag * second_real - first_real * second_imag)
        power_first = multilook(first_real * first_real + first_imag * first_imag)
        power_second = multilook(second_real * second_real + second_imag * second_imag)
        stacked = jnp.stack([look_real, look_imag, power_first, power_second])
        padded = jnp.pad(stacked, ((0, 0), (1, 1), (0, 0)))
        boxed = window_sum(padded)
        coherent = jnp.sqrt(boxed[0] ** 2 + boxed[1] ** 2) / jnp.sqrt(boxed[2] * boxed[3])
        return (coherent, jnp.arctan2(look_imag, look_real))
    coherence, phase = lax.map(per_pair, (inverse[ref_acq], inverse[sec_acq]))
    coherence = jnp.where(living[:, None, None], coherence, 0.0)
    phase = jnp.where(living[:, None, None], phase, 0.0)
    design = (numbers[None, :] == ref_acq[:, None]).astype(jnp.float32) - (numbers[None, :] == sec_acq[:, None]).astype(jnp.float32)
    design = jnp.where(living[:, None], design, 0.0)
    normal = jnp.dot(design.T, design, precision=lax.Precision.HIGHEST) + jnp.eye(NACQ, dtype=jnp.float32)
    solver = jnp.linalg.solve(normal, design.T)
    flat_phase = phase.reshape(NPAIR, NPIX)
    series = lax.dot_general(flat_phase, solver, (((0,), (1,)), ((), ())), precision=lax.Precision.HIGHEST)
    return (series, coherence)
```

```python
import functools

import jax
import jax.numpy as jnp
from jax import lax
from jax.experimental import pallas as pl
from jax.experimental.pallas import tpu as pltpu
from jax.sharding import PartitionSpec as P

MESH = pl.DeviceIdType.MESH
HIGHEST = lax.Precision.HIGHEST
NREF = 4
LOOKS = 4
NX = 4
NZ = 8
A_DEV = 4
CAP = 8
COLS = 512
BLOCKS = 4
ROWS = 8
NACQ = 128
SLOTS = NX * CAP
ACQS = NX * A_DEV
QUANT = 2 * SLOTS + NREF + ACQS
QPAD = 88

ATAN = (
    1.0, -0.33333277702331543, 0.1999807506799698, -0.1426001638174057, 0.1093234121799469,
    -0.08349724858999252, 0.05708955600857735, -0.03035186603665352, 0.010487649589776993,
    -0.0017011701129376888,
)


def atan2(y, x):
    ax, ay = jnp.abs(x), jnp.abs(y)
    t = jnp.minimum(ax, ay) / jnp.maximum(ax, ay)
    u = t * t
    acc = jnp.full_like(u, ATAN[-1])
    for coefficient in ATAN[-2::-1]:
        acc = acc * u + coefficient
    r = acc * t
    r = jnp.where(ay > ax, jnp.pi / 2 - r, r)
    r = jnp.where(x < 0, jnp.pi - r, r)
    return jnp.where(y < 0, -r, r)


def dot(a, b, dims):
    return lax.dot_general(a, b, (dims, ((), ())), precision=HIGHEST, preferred_element_type=jnp.float32)


def make_solver(design, refs):
    lane = lax.broadcasted_iota(jnp.int32, (8, NACQ), 1)
    sub = lax.broadcasted_iota(jnp.int32, (8, NACQ), 0)
    pick = jnp.zeros((8, NACQ), jnp.float32)
    for k in range(NREF):
        pick = jnp.where((sub == k) & (lane == refs[k]), 1.0, pick)
    is_ref = jnp.sum(pick, axis=0, keepdims=True)
    other = 1.0 - is_ref
    degree = jnp.sum(design * design, axis=0, keepdims=True)
    inverse = other / (1.0 + degree)
    on_ref = dot(design, pick, ((1,), (1,)))
    normal_ref = dot(on_ref, design, ((0,), (0,))) + pick
    right = on_ref - dot(design * inverse, normal_ref, ((1,), (1,)))
    schur = dot(normal_ref, pick, ((1,), (1,))) - dot(normal_ref * inverse, normal_ref, ((1,), (1,)))
    row8 = lax.broadcasted_iota(jnp.int32, (8, 8), 0)
    col8 = lax.broadcasted_iota(jnp.int32, (8, 8), 1)
    eye8 = jnp.where(row8 == col8, 1.0, 0.0)
    left = schur + jnp.where(row8 >= NREF, eye8, 0.0)
    inv = eye8
    for k in range(NREF):
        pivot = 1.0 / left[k : k + 1, k : k + 1]
        lrow, irow = left[k : k + 1, :] * pivot, inv[k : k + 1, :] * pivot
        column = jnp.where(row8[:, 0:1] == k, 0.0, left[:, k : k + 1])
        left = jnp.where(row8 == k, lrow, left - column * lrow)
        inv = jnp.where(row8 == k, irow, inv - column * irow)
    at_ref = dot(right, inv, ((1,), (0,)))
    rest = (design - dot(at_ref, normal_ref, ((1,), (0,)))) * inverse
    return rest + dot(at_ref, pick, ((1,), (0,)))


def kernel(
    chunks, nc,
    stack_hbm, pairs, order, refs, owners, series, coherence,
    stack, ps, xa, xg, zs, zr, rf, ph, pa, info, info_s, da, xt, quant, hlo, hhi, rlo, rhi, coh,
    load_sem, s1s, s1r, i_sem, is_, ir, d2s, d2r, rs_s, rs_r, ag_s, ag_r, pa_s, pa_r, h_s, h_r, co_s, co_r, own_sem,
):
    width = COLS // nc
    tile, acq = lax.axis_index("tile"), lax.axis_index("acq")
    x, z = acq // NZ, lax.rem(acq, NZ)

    def at_x(d):
        return lax.rem(x + d, NX)

    def at_z(d):
        return lax.rem(z + d, NZ)

    def dev_x(d):
        return (tile, at_x(d) * NZ + z)

    def dev_z(d):
        return (tile, x * NZ + at_z(d))

    place = tile * NX + x

    def dev_q(d):
        q = lax.rem(place + d + 32, 32)
        return (q // NX, lax.rem(q, NX) * NZ + z)

    loads = []
    for a in range(A_DEV):
        for b in range(BLOCKS):
            copy = pltpu.make_async_copy(
                stack_hbm.at[a, :, :, pl.ds(b * 128, 128)], stack.at[a, b], load_sem.at[a, b]
            )
            copy.start()
            loads.append(copy)

    barrier = pltpu.get_barrier_semaphore()
    partners = [dev_x(d) for d in range(1, NX)] + [dev_z(d) for d in range(1, NZ)] + [dev_q(1), dev_q(-1)]
    for partner in partners:
        pl.semaphore_signal(barrier, inc=1, device_id=partner, device_id_type=MESH)

    def send(src, dst, ssem, rsem, device):
        copy = pltpu.make_async_remote_copy(
            src_ref=src, dst_ref=dst, send_sem=ssem, recv_sem=rsem, device_id=device, device_id_type=MESH
        )
        copy.start()

    def wait(ref, sem):
        pltpu.make_async_copy(ref, ref, sem).wait()

    mine = [order[acq * A_DEV + a] for a in range(A_DEV)]
    ref_no = [refs[k] for k in range(NREF)]
    is_ref = []
    for a in range(A_DEV):
        hit = jnp.int32(0)
        for k in range(NREF):
            hit = hit + jnp.where(mine[a] == ref_no[k], 1, 0)
        is_ref.append(jnp.minimum(hit, 1))
    n_ref = is_ref[0] + is_ref[1] + is_ref[2] + is_ref[3]
    position, refs_before, others_before = [], jnp.int32(0), jnp.int32(0)
    for a in range(A_DEV):
        position.append(jnp.where(is_ref[a] > 0, refs_before, n_ref + others_before))
        refs_before = refs_before + is_ref[a]
        others_before = others_before + 1 - is_ref[a]
    local = []
    for c in range(A_DEV):
        where = jnp.int32(0)
        for a in range(A_DEV):
            where = where + jnp.where(position[a] == c, a, 0)
        local.append(jnp.minimum(where, A_DEV - 1))

    lane = lax.broadcasted_iota(jnp.int32, (CAP, 128), 1)
    sub = lax.broadcasted_iota(jnp.int32, (CAP, 128), 0)
    rows = jnp.zeros((CAP, 128), jnp.float32)
    facts = jnp.zeros((CAP, 128), jnp.int32)
    for s in range(CAP):
        kind, second = pairs[s, 0], pairs[s, 1]
        live = jnp.where(kind >= 0, 1, 0)
        kind = jnp.maximum(kind, 0)
        first = refs[kind]
        spot = jnp.int32(0)
        for a in range(A_DEV):
            spot = spot + jnp.where(mine[a] == second, position[a], 0)
        spot = jnp.minimum(spot, A_DEV - 1)
        row = jnp.where(lane == first, 1.0, 0.0) - jnp.where(lane == second, 1.0, 0.0)
        row = jnp.where(live > 0, row, 0.0)
        rows = jnp.where(sub == s, row, rows)
        fact = jnp.where(lane == 0, kind, jnp.where(lane == 1, spot, jnp.where(lane == 2, live, 0)))
        facts = jnp.where(sub == s, fact, facts)
    info[x] = facts
    da[z, x] = rows

    for copy in loads:
        copy.wait()

    def arrange(c):
        a = local[c]

        def body(t, carry):
            q, part = t // 2, lax.rem(t, 2)
            for j in range(LOOKS):
                for b in range(BLOCKS):
                    h, inner = divmod(b, BLOCKS // nc)
                    ps[c, q, h, part, j, :, pl.ds(inner * 128, 128)] = stack[
                        a, b, part, pl.ds(q * (ROWS * LOOKS) + j, ROWS, stride=LOOKS), :
                    ]
            return carry

        lax.fori_loop(0, NX * 2, body, 0)

    own = []

    def landing(c):
        return xa.at[c] if c < chunks else xg.at[c]

    def send_chunk(c):
        for d in (1, 3, 2):
            send(ps.at[c, at_x(d)], landing(c).at[x], s1s.at[c], s1r.at[c], dev_x(d))
        copy = pltpu.make_async_copy(ps.at[c, x], landing(c).at[x], own_sem.at[c])
        copy.start()
        own.append(copy)

    arrange(0)
    pl.semaphore_wait(barrier, len(partners))
    for d in range(1, NX):
        send(info.at[x], info.at[x], is_, ir, dev_x(d))
        send(da.at[z, x], da.at[z, x], d2s.at[0], d2r.at[0], dev_x(d))
    send_chunk(0)
    for c in range(1, A_DEV):
        arrange(c)
        send_chunk(c)

    three = pl.ds(0, NX - 1)
    wait(info.at[three], ir)
    to_smem = pltpu.make_async_copy(info, info_s, i_sem)
    to_smem.start()
    wait(da.at[0, three], d2r.at[0])
    for d in range(1, NZ):
        send(da.at[z], da.at[z], d2s.at[1], d2r.at[1], dev_z(d))

    def arrived(c):
        wait(landing(c).at[three], s1r.at[c])
        own[c].wait()

    for c in range(chunks):
        arrived(c)

    where_ref = [(owners[k], owners[NREF + k], owners[2 * NREF + k]) for k in range(NREF)]
    seven = pl.ds(0, NZ - 1)
    for h in range(nc):
        for k in range(NREF):
            rx, _, rc = where_ref[k]
            for part in range(2):
                for j in range(LOOKS):
                    zs[h, part * LOOKS + j, k] = xa[rc, rx, h, part, j]
        for d in range(1, NZ):
            send(zs.at[h, at_z(d)], zr.at[h, z], rs_s.at[h], rs_r.at[h], dev_z(d))
        zr[h, z] = zs[h, z]

    half = NREF // 2
    low, high = pl.ds(0, half), pl.ds(half, half)
    for h in range(nc):
        wait(zr.at[h, seven], rs_r.at[h])
        for k in range(NREF):
            _, rz, _ = where_ref[k]
            rf[h, z, k] = zr[h, rz, k]
        send(rf.at[h, z], rf.at[h, z], ag_s.at[h, 0, 0], ag_r.at[h, 0, 0], dev_z(1))
        send(rf.at[h, z], rf.at[h, z], ag_s.at[h, 1, 0], ag_r.at[h, 1, 0], dev_z(7))

    def take(t, carry):
        for c in range(chunks):
            for part in range(2):
                for j in range(LOOKS):
                    xg[c, t // nc, lax.rem(t, nc), part, j] = xa[c, t // nc, lax.rem(t, nc), part, j]
        return carry

    lax.fori_loop(0, NX * nc, take, 0)
    for c in range(chunks, A_DEV):
        arrived(c)
    to_smem.wait()
    wait(da.at[seven], d2r.at[1])
    xt[...] = make_solver(da[...].reshape(NZ * NX * CAP, NACQ), ref_no)

    for step in range(1, 4):
        for h in range(nc):
            left, right = at_z(NZ - step), at_z(step)
            wait(rf.at[h, left], ag_r.at[h, 0, step - 1])
            wait(rf.at[h, right], ag_r.at[h, 1, step - 1])
            if step < 3:
                send(rf.at[h, left], rf.at[h, left], ag_s.at[h, 0, step], ag_r.at[h, 0, step], dev_z(1))
                send(rf.at[h, right], rf.at[h, right], ag_s.at[h, 1, step], ag_r.at[h, 1, step], dev_z(7))
            else:
                send(rf.at[h, left, low], rf.at[h, left, low], ag_s.at[h, 0, 3], ag_r.at[h, 0, 3], dev_z(1))
                send(rf.at[h, right, high], rf.at[h, right, high], ag_s.at[h, 1, 3], ag_r.at[h, 1, 3], dev_z(7))

    for h in range(nc):
        far = at_z(4)
        wait(rf.at[h, far, low], ag_r.at[h, 0, 3])
        wait(rf.at[h, far, high], ag_r.at[h, 1, 3])
        columns = pl.ds(h * width, width)

        def slot_body(s, carry, h=h, columns=columns):
            group, index = s // CAP, lax.rem(s, CAP)
            kind, spot, live = info_s[group, index, 0], info_s[group, index, 1], info_s[group, index, 2]
            real = imag = None
            for j in range(LOOKS):
                a, b = rf[h, j, kind], rf[h, LOOKS + j, kind]
                c, d = xg[spot, group, h, 0, j], xg[spot, group, h, 1, j]
                re, im = a * c + b * d, b * c - a * d
                real, imag = (re, im) if j == 0 else (real + re, imag + im)
            quant[s, :, columns] = real
            quant[SLOTS + s, :, columns] = imag
            phase = jnp.where(live > 0, atan2(imag, real), 0.0)
            for b in range(BLOCKS // nc):
                ph[h, b, pl.ds(s, ROWS, stride=SLOTS), :] = phase[:, b * 128 : (b + 1) * 128]
            return carry

        lax.fori_loop(0, SLOTS, slot_body, 0)
        for d in range(1, NZ):
            target = at_z(d)
            block = pl.ds(pl.multiple_of(target * SLOTS, SLOTS), SLOTS)
            mine_there = pl.ds(pl.multiple_of(z * SLOTS, SLOTS), SLOTS)
            send(ph.at[h, :, block], pa.at[h, :, mine_there], pa_s.at[h], pa_r.at[h], dev_z(d))
        here = pl.ds(pl.multiple_of(z * SLOTS, SLOTS), SLOTS)
        pa[h, :, here] = ph[h, :, here]

    for h in range(nc):
        columns = pl.ds(h * width, width)
        for k in range(NREF):
            total = None
            for j in range(LOOKS):
                a, b = rf[h, j, k], rf[h, LOOKS + j, k]
                term = a * a + b * b
                total = term if j == 0 else total + term
            quant[2 * SLOTS + k, :, columns] = total

        def power_body(s, carry, h=h, columns=columns):
            total = None
            for j in range(LOOKS):
                c, d = xg[lax.rem(s, A_DEV), s // A_DEV, h, 0, j], xg[lax.rem(s, A_DEV), s // A_DEV, h, 1, j]
                term = c * c + d * d
                total = term if j == 0 else total + term
            quant[2 * SLOTS + NREF + s, :, columns] = total
            return carry

        lax.fori_loop(0, ACQS, power_body, 0)

    col = lax.broadcasted_iota(jnp.int32, (ROWS, COLS), 1)
    row = lax.broadcasted_iota(jnp.int32, (ROWS, COLS), 0)

    def moved(v, by):
        out = pltpu.roll(v, by % COLS, 1)
        return jnp.where(col >= by, out, 0.0) if by > 0 else jnp.where(col < COLS + by, out, 0.0)

    def column_body(q, carry):
        v = quant[q]
        v = v + moved(v, 1) + moved(v, 2) + moved(v, -1) + moved(v, -2)
        quant[q] = v
        hlo[pl.ds(q, 1), :] = v[0:1, :]
        hhi[pl.ds(q, 1), :] = v[ROWS - 1 : ROWS, :]
        return carry

    lax.fori_loop(0, QUANT, column_body, 0)
    for rest in (hlo, hhi):
        rest[QUANT:QPAD, :] = jnp.zeros((QPAD - QUANT, COLS), jnp.float32)
    send(hlo, rhi, h_s.at[0], h_r.at[0], dev_q(-1))
    send(hhi, rlo, h_s.at[1], h_r.at[1], dev_q(1))
    wait(rhi, h_r.at[0])
    wait(rlo, h_r.at[1])
    below = jnp.where(place > 0, 1.0, 0.0)
    above = jnp.where(place < 31, 1.0, 0.0)

    def boxed(q):
        v = quant[q]
        down = jnp.where(row == 0, rlo[pl.ds(q, 1), :] * below, pltpu.roll(v, 1, 0))
        up = jnp.where(row == ROWS - 1, rhi[pl.ds(q, 1), :] * above, pltpu.roll(v, ROWS - 1, 0))
        return v + down + up

    def power_box(q, carry):
        quant[2 * SLOTS + q] = boxed(2 * SLOTS + q)
        return carry

    lax.fori_loop(0, NREF + ACQS, power_box, 0)

    def coherence_body(s, carry):
        group, index = s // CAP, lax.rem(s, CAP)
        kind, spot, live = info_s[group, index, 0], info_s[group, index, 1], info_s[group, index, 2]
        real, imag = boxed(s), boxed(SLOTS + s)
        first = quant[2 * SLOTS + kind]
        second = quant[2 * SLOTS + NREF + group * A_DEV + spot]
        value = jnp.sqrt(real * real + imag * imag) / jnp.sqrt(first * second)
        coh[group, index] = jnp.where(live > 0, value, 0.0)
        return carry

    lax.fori_loop(0, SLOTS, coherence_body, 0)
    quarter = pl.ds(pl.multiple_of(x * ROWS, ROWS), ROWS)
    for d in range(1, NX):
        send(coh.at[at_x(d)], coherence.at[:, quarter, :], co_s, co_r, dev_x(d))
    coherence[:, quarter, :] = coh[x]

    for h in range(nc):
        wait(pa.at[h, :, pl.ds(0, (NZ - 1) * SLOTS)], pa_r.at[h])
        for b in range(BLOCKS // nc):
            series[pl.ds(h * width + b * 128, 128), :] = dot(pa[h, b], xt[...], ((0,), (0,)))

    wait(coh.at[three], co_r)
    wait(coh.at[three], co_s)
    wait(info.at[three], is_)
    wait(da.at[0, three], d2s.at[0])
    wait(da.at[seven], d2s.at[1])
    for c in range(A_DEV):
        wait(ps.at[c, three], s1s.at[c])
    for h in range(nc):
        wait(zs.at[h, seven], rs_s.at[h])
        wait(pa.at[h, :, pl.ds(0, (NZ - 1) * SLOTS)], pa_s.at[h])
        for way in range(2):
            for step in range(3):
                wait(rf.at[h, 0], ag_s.at[h, way, step])
            wait(rf.at[h, 0, low], ag_s.at[h, way, 3])
    wait(hlo, h_s.at[0])
    wait(hhi, h_s.at[1])


def call(chunks, nc, cid, stack, pairs, order, refs, owners):
    width = COLS // nc
    f32 = jnp.float32
    dma = pltpu.SemaphoreType.DMA
    smem = pl.BlockSpec(memory_space=pltpu.SMEM)
    vmem = pl.BlockSpec(memory_space=pltpu.VMEM)
    return pl.pallas_call(
        functools.partial(kernel, chunks, nc),
        out_shape=(
            jax.ShapeDtypeStruct((COLS, NACQ), f32),
            jax.ShapeDtypeStruct((CAP, NX * ROWS, COLS), f32),
        ),
        in_specs=[pl.BlockSpec(memory_space=pl.ANY), smem, smem, smem, smem],
        out_specs=(vmem, vmem),
        scratch_shapes=[
            pltpu.VMEM((A_DEV, BLOCKS, 2, NX * ROWS * LOOKS, 128), f32),
            pltpu.VMEM((A_DEV, NX, nc, 2, LOOKS, ROWS, width), f32),
            pltpu.VMEM((chunks, NX, nc, 2, LOOKS, ROWS, width), f32),
            pltpu.VMEM((A_DEV, NX, nc, 2, LOOKS, ROWS, width), f32),
            pltpu.VMEM((nc, NZ, NREF, ROWS, width), f32),
            pltpu.VMEM((nc, NZ, NREF, ROWS, width), f32),
            pltpu.VMEM((nc, NZ, NREF, ROWS, width), f32),
            pltpu.VMEM((nc, BLOCKS // nc, ROWS * SLOTS, 128), f32),
            pltpu.VMEM((nc, BLOCKS // nc, NZ * SLOTS, 128), f32),
            pltpu.VMEM((NX, CAP, 128), jnp.int32),
            pltpu.SMEM((NX, CAP, 128), jnp.int32),
            pltpu.VMEM((NZ, NX, CAP, NACQ), f32),
            pltpu.VMEM((NZ * NX * CAP, NACQ), f32),
            pltpu.VMEM((QUANT, ROWS, COLS), f32),
            pltpu.VMEM((QPAD, COLS), f32),
            pltpu.VMEM((QPAD, COLS), f32),
            pltpu.VMEM((QPAD, COLS), f32),
            pltpu.VMEM((QPAD, COLS), f32),
            pltpu.VMEM((NX, CAP, ROWS, COLS), f32),
            dma((A_DEV, BLOCKS)), dma((A_DEV,)), dma((A_DEV,)), dma, dma, dma, dma((2,)), dma((2,)),
            dma((nc,)), dma((nc,)), dma((nc, 2, 4)), dma((nc, 2, 4)), dma((nc,)), dma((nc,)),
            dma((2,)), dma((2,)), dma, dma, dma((A_DEV,)),
        ],
        compiler_params=pltpu.CompilerParams(
            collective_id=cid, has_side_effects=True, vmem_limit_bytes=48 << 20
        ),
        name=f"sbas{chunks}",
    )(stack, pairs, order, refs, owners)


def local(stack, pairs, order, refs):
    numbers = jnp.arange(NACQ, dtype=jnp.int32)
    slot = jnp.sum(jnp.where(order[None, :] == refs[:, None], numbers[None, :], 0), axis=1)
    owner = slot // A_DEV
    before = (owner[None, :] == owner[:, None]) & (slot[None, :] < slot[:, None])
    chunk = jnp.sum(before.astype(jnp.int32), axis=1)
    owners = jnp.concatenate([owner // NZ, owner % NZ, chunk]).astype(jnp.int32)
    crowd = jnp.max(chunk)
    variants = [functools.partial(call, 1, NC, 1), functools.partial(call, 2, NC, 2), functools.partial(call, 4, NC, 3)]
    pick = jnp.minimum(crowd, 2)
    return lax.switch(pick, variants, stack, pairs, order, refs, owners)


NC = 1


def solution(mesh):
    return jax.shard_map(
        local,
        mesh=mesh,
        in_specs=(P("acq", None, "tile", None), P("acq", None), P(), P()),
        out_specs=(P(("tile", "acq"), None), P("acq", "tile", None)),
        check_vma=False,
    )
```

```python
import functools

import jax
import jax.numpy as jnp
from jax import lax
from jax.experimental import pallas as pl
from jax.experimental.pallas import tpu as pltpu
from jax.sharding import PartitionSpec as P

MESH = pl.DeviceIdType.MESH
HIGHEST = lax.Precision.HIGHEST
NREF = 4
LOOKS = 4
NX = 4
NZ = 8
A_DEV = 4
CAP = 8
COLS = 512
BLOCKS = 4
ROWS = 8
NACQ = 128
SLOTS = NX * CAP
ACQS = NX * A_DEV
QUANT = 2 * SLOTS + NREF + ACQS
QPAD = 88

ATAN = (
    1.0, -0.33333277702331543, 0.1999807506799698, -0.1426001638174057, 0.1093234121799469,
    -0.08349724858999252, 0.05708955600857735, -0.03035186603665352, 0.010487649589776993,
    -0.0017011701129376888,
)


def atan2(y, x):
    ax, ay = jnp.abs(x), jnp.abs(y)
    t = jnp.minimum(ax, ay) / jnp.maximum(ax, ay)
    u = t * t
    acc = jnp.full_like(u, ATAN[-1])
    for coefficient in ATAN[-2::-1]:
        acc = acc * u + coefficient
    r = acc * t
    r = jnp.where(ay > ax, jnp.pi / 2 - r, r)
    r = jnp.where(x < 0, jnp.pi - r, r)
    return jnp.where(y < 0, -r, r)


def dot(a, b, dims):
    return lax.dot_general(a, b, (dims, ((), ())), precision=HIGHEST, preferred_element_type=jnp.float32)


def make_solver(design, refs):
    lane = lax.broadcasted_iota(jnp.int32, (8, NACQ), 1)
    sub = lax.broadcasted_iota(jnp.int32, (8, NACQ), 0)
    pick = jnp.zeros((8, NACQ), jnp.float32)
    for k in range(NREF):
        pick = jnp.where((sub == k) & (lane == refs[k]), 1.0, pick)
    is_ref = jnp.sum(pick, axis=0, keepdims=True)
    other = 1.0 - is_ref
    degree = jnp.sum(design * design, axis=0, keepdims=True)
    inverse = other / (1.0 + degree)
    on_ref = dot(design, pick, ((1,), (1,)))
    normal_ref = dot(on_ref, design, ((0,), (0,))) + pick
    right = on_ref - dot(design * inverse, normal_ref, ((1,), (1,)))
    schur = dot(normal_ref, pick, ((1,), (1,))) - dot(normal_ref * inverse, normal_ref, ((1,), (1,)))
    row8 = lax.broadcasted_iota(jnp.int32, (8, 8), 0)
    col8 = lax.broadcasted_iota(jnp.int32, (8, 8), 1)
    eye8 = jnp.where(row8 == col8, 1.0, 0.0)
    left = schur + jnp.where(row8 >= NREF, eye8, 0.0)
    inv = eye8
    for k in range(NREF):
        pivot = 1.0 / left[k : k + 1, k : k + 1]
        lrow, irow = left[k : k + 1, :] * pivot, inv[k : k + 1, :] * pivot
        column = jnp.where(row8[:, 0:1] == k, 0.0, left[:, k : k + 1])
        left = jnp.where(row8 == k, lrow, left - column * lrow)
        inv = jnp.where(row8 == k, irow, inv - column * irow)
    at_ref = dot(right, inv, ((1,), (0,)))
    rest = (design - dot(at_ref, normal_ref, ((1,), (0,)))) * inverse
    return rest + dot(at_ref, pick, ((1,), (0,)))


def kernel(
    chunks, nc,
    stack_hbm, pairs, order, refs, series, coherence,
    stack, ps, xg, zs, zr, yx, yr, rf, ph, pa, info, info_s, da, xt, quant, hlo, hhi, rlo, rhi, coh,
    load_sem, s1s, s1r, i_sem, is_, ir, d2s, d2r, rs_s, rs_r, y_s, y_r, ag_s, ag_r, pa_s, pa_r, h_s, h_r, co_s, co_r, own_sem,
):
    width = COLS // nc
    tile, acq = lax.axis_index("tile"), lax.axis_index("acq")
    x, z = acq // NZ, lax.rem(acq, NZ)

    def at_x(d):
        return lax.rem(x + d, NX)

    def at_z(d):
        return lax.rem(z + d, NZ)

    def dev_x(d):
        return (tile, at_x(d) * NZ + z)

    def dev_z(d):
        return (tile, x * NZ + at_z(d))

    place = tile * NX + x

    def dev_q(d):
        q = lax.rem(place + d + 32, 32)
        return (q // NX, lax.rem(q, NX) * NZ + z)

    loads = []
    for a in range(A_DEV):
        for b in range(BLOCKS):
            copy = pltpu.make_async_copy(
                stack_hbm.at[a, :, :, pl.ds(b * 128, 128)], stack.at[a, b], load_sem.at[a, b]
            )
            copy.start()
            loads.append(copy)

    barrier = pltpu.get_barrier_semaphore()
    partners = [dev_x(d) for d in range(1, NX)] + [dev_z(d) for d in range(1, NZ)] + [dev_q(1), dev_q(-1)]
    for partner in partners:
        pl.semaphore_signal(barrier, inc=1, device_id=partner, device_id_type=MESH)

    def send(src, dst, ssem, rsem, device):
        copy = pltpu.make_async_remote_copy(
            src_ref=src, dst_ref=dst, send_sem=ssem, recv_sem=rsem, device_id=device, device_id_type=MESH
        )
        copy.start()

    def wait(ref, sem):
        pltpu.make_async_copy(ref, ref, sem).wait()

    mine = [order[acq * A_DEV + a] for a in range(A_DEV)]
    ref_no = [refs[k] for k in range(NREF)]
    is_ref = []
    for a in range(A_DEV):
        hit = jnp.int32(0)
        for k in range(NREF):
            hit = hit + jnp.where(mine[a] == ref_no[k], 1, 0)
        is_ref.append(jnp.minimum(hit, 1))
    n_ref = is_ref[0] + is_ref[1] + is_ref[2] + is_ref[3]
    position, refs_before, others_before = [], jnp.int32(0), jnp.int32(0)
    for a in range(A_DEV):
        position.append(jnp.where(is_ref[a] > 0, refs_before, n_ref + others_before))
        refs_before = refs_before + is_ref[a]
        others_before = others_before + 1 - is_ref[a]
    local = []
    for c in range(A_DEV):
        where = jnp.int32(0)
        for a in range(A_DEV):
            where = where + jnp.where(position[a] == c, a, 0)
        local.append(jnp.minimum(where, A_DEV - 1))

    lane = lax.broadcasted_iota(jnp.int32, (CAP, 128), 1)
    sub = lax.broadcasted_iota(jnp.int32, (CAP, 128), 0)
    rows = jnp.zeros((CAP, 128), jnp.float32)
    facts = jnp.zeros((CAP, 128), jnp.int32)
    for s in range(CAP):
        kind, second = pairs[s, 0], pairs[s, 1]
        live = jnp.where(kind >= 0, 1, 0)
        kind = jnp.maximum(kind, 0)
        first = refs[kind]
        spot = jnp.int32(0)
        for a in range(A_DEV):
            spot = spot + jnp.where(mine[a] == second, a, 0)
        spot = jnp.minimum(spot, A_DEV - 1)
        row = jnp.where(lane == first, 1.0, 0.0) - jnp.where(lane == second, 1.0, 0.0)
        row = jnp.where(live > 0, row, 0.0)
        rows = jnp.where(sub == s, row, rows)
        fact = jnp.where(lane == 0, kind, jnp.where(lane == 1, spot, jnp.where(lane == 2, live, 0)))
        facts = jnp.where(sub == s, fact, facts)
    info[x] = facts
    da[z, x] = rows

    for copy in loads:
        copy.wait()

    def arrange(c):
        def body(t, carry):
            q, part = t // 2, lax.rem(t, 2)
            for j in range(LOOKS):
                for b in range(BLOCKS):
                    h, inner = divmod(b, BLOCKS // nc)
                    ps[c, q, h, part, j, :, pl.ds(inner * 128, 128)] = stack[
                        c, b, part, pl.ds(q * (ROWS * LOOKS) + j, ROWS, stride=LOOKS), :
                    ]
            return carry

        lax.fori_loop(0, NX * 2, body, 0)

    own = {}
    three, seven = pl.ds(0, NX - 1), pl.ds(0, NZ - 1)

    def send_chunk(c, h):
        for d in (1, 3, 2):
            send(ps.at[c, at_x(d), h], xg[h].at[c, x], s1s.at[c, h], s1r.at[c, h], dev_x(d))
        own[c, h] = pltpu.make_async_copy(ps.at[c, x, h], xg[h].at[c, x], own_sem.at[c, h])
        own[c, h].start()

    def sent(c, h):
        wait(ps.at[c, three, h], s1s.at[c, h])

    def arrived(c, h):
        wait(xg[h].at[c, three], s1r.at[c, h])
        own[c, h].wait()

    def scatter_fill():
        for r in range(chunks):
            def body(q, carry, r=r):
                for part in range(2):
                    for j in range(LOOKS):
                        for b in range(BLOCKS):
                            zs[part * LOOKS + j, r, q, :, pl.ds(b * 128, 128)] = stack[
                                local[r], b, part, pl.ds(q * (ROWS * LOOKS) + j, ROWS, stride=LOOKS), :
                            ]
                return carry

            lax.fori_loop(0, NX, body, 0)

    def scatter():
        for d in (4, 3, 5, 2, 6, 1, 7):
            send(zs.at[at_z(d)], zr.at[z], rs_s, rs_r, dev_z(d))
        zr[z] = zs[z]

    def find(n, slots):
        return tuple(slots[k] + jnp.where(order[n] == ref_no[k], n, 0) for k in range(NREF))

    def scatter_x(where_ref):
        wait(zr.at[seven], rs_r)
        for k in range(NREF):
            _, rz, rank = where_ref[k]
            for q in range(NX):
                yx[q, k] = zr[rz, rank, q]
        for d in (2, 1, 3):
            send(yx.at[at_x(d)], yr.at[x], y_s, y_r, dev_x(d))
        yr[x] = yx[x]

    half = NREF // 2
    halves = (pl.ds(0, half), pl.ds(half, half))

    def sign(way, d):
        return d if way == 0 else NZ - d

    def gather_first(h, where_ref):
        wait(yr.at[three], y_r)
        for k in range(NREF):
            rf[h][z, k] = yr[where_ref[k][0], k]
        for d in (2, 1):
            for way in range(2):
                send(
                    rf[h].at[z], rf[h].at[z], ag_s.at[h, way, d - 1], ag_r.at[h, way, d - 1], dev_z(sign(way, d))
                )

    def gather_second(h):
        for way in range(2):
            origin = at_z(sign(way, NZ - 2))
            wait(rf[h].at[origin], ag_r.at[h, way, 1])
            send(rf[h].at[origin], rf[h].at[origin], ag_s.at[h, way, 2], ag_r.at[h, way, 2], dev_z(sign(way, 1)))
            part = rf[h].at[origin, halves[way]]
            send(part, part, ag_s.at[h, way, 3], ag_r.at[h, way, 3], dev_z(sign(way, 2)))

    def gathered(h):
        for way in range(2):
            wait(rf[h].at[0], ag_r.at[h, way, 0])
            wait(rf[h].at[0], ag_r.at[h, way, 2])
            wait(rf[h].at[0, halves[way]], ag_r.at[h, way, 3])

    def solve():
        wait(da.at[seven], d2r.at[1])
        xt[...] = make_solver(da[...].reshape(NZ * NX * CAP, NACQ), ref_no)

    def facts_around():
        wait(info.at[three], ir)
        to_smem = pltpu.make_async_copy(info, info_s, i_sem)
        to_smem.start()
        wait(da.at[0, three], d2r.at[0])
        for d in range(1, NZ):
            send(da.at[z], da.at[z], d2s.at[1], d2r.at[1], dev_z(d))
        to_smem.wait()

    scatter_fill()
    pl.semaphore_wait(barrier, len(partners))
    scatter()
    for d in range(1, NX):
        send(info.at[x], info.at[x], is_, ir, dev_x(d))
        send(da.at[z, x], da.at[z, x], d2s.at[0], d2r.at[0], dev_x(d))
    for c in range(2):
        arrange(c)
        send_chunk(c, 0)
    for c in range(2, A_DEV):
        arrange(c)
    slots = lax.fori_loop(0, NACQ, find, (jnp.int32(0),) * NREF)
    slots = [jnp.minimum(slot, NACQ - 1) for slot in slots]
    owner = [lax.shift_right_logical(slot, 2) for slot in slots]
    where_ref = []
    for k in range(NREF):
        rank = jnp.int32(0)
        for other in range(NREF):
            if other != k:
                rank = rank + jnp.where((owner[other] == owner[k]) & (slots[other] < slots[k]), 1, 0)
        where_ref.append(
            (lax.shift_right_logical(owner[k], 3), lax.rem(owner[k], NZ), jnp.minimum(rank, chunks - 1))
        )
    facts_around()
    scatter_x(where_ref)
    wait(yx.at[three], y_s)
    for c in range(2, A_DEV):
        send_chunk(c, 0)
    gather_first(0, where_ref)
    gather_second(0)
    solve()

    def keep(q, v, columns):
        quant[q, :, columns] = v
        hlo[pl.ds(q, 1), columns] = v[0:1, :]
        hhi[pl.ds(q, 1), columns] = v[ROWS - 1 : ROWS, :]

    def powers(h):
        columns = pl.ds(h * width, width)
        for k in range(NREF):
            total = None
            for j in range(LOOKS):
                a, b = rf[h][j, k], rf[h][LOOKS + j, k]
                term = a * a + b * b
                total = term if j == 0 else total + term
            keep(2 * SLOTS + k, total, columns)

        def power_body(s, carry):
            total = None
            for j in range(LOOKS):
                c, d = xg[h][lax.rem(s, A_DEV), s // A_DEV, 0, j], xg[h][lax.rem(s, A_DEV), s // A_DEV, 1, j]
                term = c * c + d * d
                total = term if j == 0 else total + term
            keep(2 * SLOTS + NREF + s, total, columns)
            return carry

        lax.fori_loop(0, ACQS, power_body, 0)

    def interferograms(h):
        gathered(h)
        for c in range(A_DEV):
            arrived(c, h)
        powers(h)
        columns = pl.ds(h * width, width)

        def slot_body(s, carry):
            group, index = s // CAP, lax.rem(s, CAP)
            kind, spot, live = info_s[group, index, 0], info_s[group, index, 1], info_s[group, index, 2]
            real = imag = None
            for j in range(LOOKS):
                a, b = rf[h][j, kind], rf[h][LOOKS + j, kind]
                c, d = xg[h][spot, group, 0, j], xg[h][spot, group, 1, j]
                re, im = a * c + b * d, b * c - a * d
                real, imag = (re, im) if j == 0 else (real + re, imag + im)
            for q, v in ((s, real), (SLOTS + s, imag)):
                keep(q, v, columns)
            phase = jnp.where(live > 0, atan2(imag, real), 0.0)
            for b in range(BLOCKS // nc):
                ph[h, b, pl.ds(s, ROWS, stride=SLOTS), :] = phase[:, b * 128 : (b + 1) * 128]
            return carry

        lax.fori_loop(0, SLOTS, slot_body, 0)
        for rest in (hlo, hhi):
            rest[QUANT:QPAD, columns] = jnp.zeros((QPAD - QUANT, width), jnp.float32)
        send(hlo.at[:, columns], rhi.at[:, columns], h_s.at[0, h], h_r.at[0, h], dev_q(-1))
        send(hhi.at[:, columns], rlo.at[:, columns], h_s.at[1, h], h_r.at[1, h], dev_q(1))
        for d in range(1, NZ):
            target = at_z(d)
            block = pl.ds(pl.multiple_of(target * SLOTS, SLOTS), SLOTS)
            mine_there = pl.ds(pl.multiple_of(z * SLOTS, SLOTS), SLOTS)
            send(ph.at[h, :, block], pa.at[h, :, mine_there], pa_s.at[h], pa_r.at[h], dev_z(d))
        here = pl.ds(pl.multiple_of(z * SLOTS, SLOTS), SLOTS)
        pa[h, :, here] = ph[h, :, here]

    for h in range(nc):
        interferograms(h)

    col = lax.broadcasted_iota(jnp.int32, (ROWS, COLS), 1)
    row = lax.broadcasted_iota(jnp.int32, (ROWS, COLS), 0)

    def five(v):
        out = v
        for by in (1, 2):
            out = out + jnp.where(col >= by, pltpu.roll(v, by, 1), 0.0)
            out = out + jnp.where(col < COLS - by, pltpu.roll(v, COLS - by, 1), 0.0)
        return out

    def column_body(t, carry):
        values = [five(quant[4 * t + i]) for i in range(4)]
        for i in range(4):
            quant[4 * t + i] = values[i]
        return carry

    lax.fori_loop(0, QUANT // 4, column_body, 0)
    for h in range(nc):
        columns = pl.ds(h * width, width)
        wait(rhi.at[:, columns], h_r.at[0, h])
        wait(rlo.at[:, columns], h_r.at[1, h])
    below = jnp.where(place > 0, 1.0, 0.0)
    above = jnp.where(place < 31, 1.0, 0.0)

    def halo_body(t, carry):
        block = pl.ds(pl.multiple_of(t * 8, 8), 8)
        lo, hi = five(rlo[block, :]) * below, five(rhi[block, :]) * above
        rlo[block, :], rhi[block, :] = lo, hi
        return carry

    lax.fori_loop(0, QPAD // 8, halo_body, 0)

    def boxed(q):
        v = quant[q]
        down = jnp.where(row == 0, rlo[pl.ds(q, 1), :], pltpu.roll(v, 1, 0))
        up = jnp.where(row == ROWS - 1, rhi[pl.ds(q, 1), :], pltpu.roll(v, ROWS - 1, 0))
        return v + down + up

    def power_box(t, carry):
        values = [boxed(2 * SLOTS + 4 * t + i) for i in range(4)]
        for i in range(4):
            quant[2 * SLOTS + 4 * t + i] = values[i]
        return carry

    lax.fori_loop(0, (NREF + ACQS) // 4, power_box, 0)
    quarter = pl.ds(pl.multiple_of(x * ROWS, ROWS), ROWS)
    for d in (2, 1, 3, 0):
        group = at_x(d)

        def coherence_body(t, carry, group=group):
            values = []
            for i in range(2):
                index = 2 * t + i
                s = group * CAP + index
                kind, spot, live = info_s[group, index, 0], info_s[group, index, 1], info_s[group, index, 2]
                real, imag = boxed(s), boxed(SLOTS + s)
                first = quant[2 * SLOTS + kind]
                second = quant[2 * SLOTS + NREF + group * A_DEV + spot]
                value = jnp.sqrt(real * real + imag * imag) / jnp.sqrt(first * second)
                values.append(jnp.where(live > 0, value, 0.0))
            for i in range(2):
                coh[group, 2 * t + i] = values[i]
            return carry

        lax.fori_loop(0, CAP // 2, coherence_body, 0)
        if d:
            send(coh.at[group], coherence.at[:, quarter, :], co_s, co_r, dev_x(d))
    coherence[:, quarter, :] = coh[x]

    for h in range(nc):
        wait(pa.at[h, :, pl.ds(0, (NZ - 1) * SLOTS)], pa_r.at[h])
        for b in range(BLOCKS // nc):
            series[pl.ds(h * width + b * 128, 128), :] = dot(pa[h, b], xt[...], ((0,), (0,)))

    wait(coh.at[three], co_r)
    wait(coh.at[three], co_s)
    wait(info.at[three], is_)
    wait(da.at[0, three], d2s.at[0])
    wait(da.at[seven], d2s.at[1])
    for h in range(nc):
        for c in range(A_DEV):
            sent(c, h)
        wait(zs.at[seven], rs_s)
        wait(pa.at[h, :, pl.ds(0, (NZ - 1) * SLOTS)], pa_s.at[h])
        for way in range(2):
            for step in range(3):
                wait(rf[h].at[0], ag_s.at[h, way, step])
            wait(rf[h].at[0, halves[way]], ag_s.at[h, way, 3])
        columns = pl.ds(h * width, width)
        wait(hlo.at[:, columns], h_s.at[0, h])
        wait(hhi.at[:, columns], h_s.at[1, h])


def call(chunks, nc, cid, stack, pairs, order, refs):
    width = COLS // nc
    f32 = jnp.float32
    dma = pltpu.SemaphoreType.DMA
    smem = pl.BlockSpec(memory_space=pltpu.SMEM)
    vmem = pl.BlockSpec(memory_space=pltpu.VMEM)
    return pl.pallas_call(
        functools.partial(kernel, chunks, nc),
        out_shape=(
            jax.ShapeDtypeStruct((COLS, NACQ), f32),
            jax.ShapeDtypeStruct((CAP, NX * ROWS, COLS), f32),
        ),
        in_specs=[pl.BlockSpec(memory_space=pl.ANY), smem, smem, smem],
        out_specs=(vmem, vmem),
        scratch_shapes=[
            pltpu.VMEM((A_DEV, BLOCKS, 2, NX * ROWS * LOOKS, 128), f32),
            pltpu.VMEM((A_DEV, NX, nc, 2, LOOKS, ROWS, width), f32),
            [pltpu.VMEM((A_DEV, NX, 2, LOOKS, ROWS, width), f32)] * nc,
            pltpu.VMEM((NZ, chunks, NX, ROWS, COLS), f32),
            pltpu.VMEM((NZ, chunks, NX, ROWS, COLS), f32),
            pltpu.VMEM((NX, NREF, ROWS, COLS), f32),
            pltpu.VMEM((NX, NREF, ROWS, COLS), f32),
            [pltpu.VMEM((NZ, NREF, ROWS, width), f32)] * nc,
            pltpu.VMEM((nc, BLOCKS // nc, ROWS * SLOTS, 128), f32),
            pltpu.VMEM((nc, BLOCKS // nc, NZ * SLOTS, 128), f32),
            pltpu.VMEM((NX, CAP, 128), jnp.int32),
            pltpu.SMEM((NX, CAP, 128), jnp.int32),
            pltpu.VMEM((NZ, NX, CAP, NACQ), f32),
            pltpu.VMEM((NZ * NX * CAP, NACQ), f32),
            pltpu.VMEM((QUANT, ROWS, COLS), f32),
            pltpu.VMEM((QPAD, COLS), f32),
            pltpu.VMEM((QPAD, COLS), f32),
            pltpu.VMEM((QPAD, COLS), f32),
            pltpu.VMEM((QPAD, COLS), f32),
            pltpu.VMEM((NX, CAP, ROWS, COLS), f32),
            dma((A_DEV, BLOCKS)), dma((A_DEV, nc)), dma((A_DEV, nc)), dma, dma, dma, dma((2,)), dma((2,)),
            dma, dma, dma, dma, dma((nc, 2, 4)), dma((nc, 2, 4)), dma((nc,)), dma((nc,)),
            dma((2, nc)), dma((2, nc)), dma, dma, dma((A_DEV, nc)),
        ],
        compiler_params=pltpu.CompilerParams(
            collective_id=cid, has_side_effects=True, vmem_limit_bytes=48 << 20
        ),
        name=f"sbas{chunks}",
    )(stack, pairs, order, refs)


def local(stack, pairs, order, refs):
    numbers = lax.broadcasted_iota(jnp.int32, (NACQ, NACQ), 0) // A_DEV
    across = lax.broadcasted_iota(jnp.int32, (NACQ, NACQ), 1) // A_DEV
    rows = lax.broadcast_in_dim(order, (NACQ, NACQ), (0,))
    columns = lax.broadcast_in_dim(order, (NACQ, NACQ), (1,))
    one = [refs[k] for k in range(NREF)]
    held = (rows == one[0]) | (rows == one[1]) | (rows == one[2]) | (rows == one[3])
    also = (columns == one[0]) | (columns == one[1]) | (columns == one[2]) | (columns == one[3])
    together = jnp.sum((held & also & (numbers == across)).astype(jnp.int32))
    pick = jnp.where(together > 8, 2, jnp.where(together > 4, 1, 0))
    variants = [functools.partial(call, 1, NC, 1), functools.partial(call, 2, NC, 2), functools.partial(call, 4, NC, 3)]
    return lax.switch(pick, variants, stack, pairs, order, refs)


NC = 1


def solution(mesh):
    return jax.shard_map(
        local,
        mesh=mesh,
        in_specs=(P("acq", None, "tile", None), P("acq", None), P(), P()),
        out_specs=(P(("tile", "acq"), None), P("acq", "tile", None)),
        check_vma=False,
    )
```

```python
import functools

import jax
import jax.numpy as jnp
from jax import lax
from jax.experimental import pallas as pl
from jax.experimental.pallas import tpu as pltpu
from jax.sharding import PartitionSpec as P

MESH = pl.DeviceIdType.MESH
HIGHEST = lax.Precision.HIGHEST
NREF = 4
LOOKS = 4
NX = 4
NZ = 8
A_DEV = 4
CAP = 8
COLS = 512
BLOCKS = 4
ROWS = 8
NACQ = 128
SLOTS = NX * CAP
ACQS = NX * A_DEV
QUANT = 2 * SLOTS + NREF + ACQS
QPAD = 88

ATAN = (
    1.0, -0.33333277702331543, 0.1999807506799698, -0.1426001638174057, 0.1093234121799469,
    -0.08349724858999252, 0.05708955600857735, -0.03035186603665352, 0.010487649589776993,
    -0.0017011701129376888,
)


def atan2(y, x):
    ax, ay = jnp.abs(x), jnp.abs(y)
    t = jnp.minimum(ax, ay) / jnp.maximum(ax, ay)
    u = t * t
    acc = jnp.full_like(u, ATAN[-1])
    for coefficient in ATAN[-2::-1]:
        acc = acc * u + coefficient
    r = acc * t
    r = jnp.where(ay > ax, jnp.pi / 2 - r, r)
    r = jnp.where(x < 0, jnp.pi - r, r)
    return jnp.where(y < 0, -r, r)


def dot(a, b, dims):
    return lax.dot_general(a, b, (dims, ((), ())), precision=HIGHEST, preferred_element_type=jnp.float32)


def make_solver(design, refs):
    lane = lax.broadcasted_iota(jnp.int32, (8, NACQ), 1)
    sub = lax.broadcasted_iota(jnp.int32, (8, NACQ), 0)
    pick = jnp.zeros((8, NACQ), jnp.float32)
    for k in range(NREF):
        pick = jnp.where((sub == k) & (lane == refs[k]), 1.0, pick)
    is_ref = jnp.sum(pick, axis=0, keepdims=True)
    other = 1.0 - is_ref
    degree = jnp.sum(design * design, axis=0, keepdims=True)
    inverse = other / (1.0 + degree)
    on_ref = dot(design, pick, ((1,), (1,)))
    normal_ref = dot(on_ref, design, ((0,), (0,))) + pick
    right = on_ref - dot(design * inverse, normal_ref, ((1,), (1,)))
    schur = dot(normal_ref, pick, ((1,), (1,))) - dot(normal_ref * inverse, normal_ref, ((1,), (1,)))
    row8 = lax.broadcasted_iota(jnp.int32, (8, 8), 0)
    col8 = lax.broadcasted_iota(jnp.int32, (8, 8), 1)
    eye8 = jnp.where(row8 == col8, 1.0, 0.0)
    left = schur + jnp.where(row8 >= NREF, eye8, 0.0)
    inv = eye8
    for k in range(NREF):
        pivot = 1.0 / left[k : k + 1, k : k + 1]
        lrow, irow = left[k : k + 1, :] * pivot, inv[k : k + 1, :] * pivot
        column = jnp.where(row8[:, 0:1] == k, 0.0, left[:, k : k + 1])
        left = jnp.where(row8 == k, lrow, left - column * lrow)
        inv = jnp.where(row8 == k, irow, inv - column * irow)
    at_ref = dot(right, inv, ((1,), (0,)))
    rest = (design - dot(at_ref, normal_ref, ((1,), (0,)))) * inverse
    return rest + dot(at_ref, pick, ((1,), (0,)))


def kernel(
    chunks, nc,
    stack_hbm, pairs, order, refs, series, coherence,
    stack, ps, xg, zs, zr, yx, yr, rf, ph, pa, info, info_s, da, xt, quant, hlo, hhi, rlo, rhi, coh,
    load_sem, s1s, s1r, i_sem, is_, ir, d2s, d2r, rs_s, rs_r, y_s, y_r, ag_s, ag_r, pa_s, pa_r, h_s, h_r, co_s, co_r, own_sem,
):
    width = COLS // nc
    tile, acq = lax.axis_index("tile"), lax.axis_index("acq")
    x, z = acq // NZ, lax.rem(acq, NZ)

    def at_x(d):
        return lax.rem(x + d, NX)

    def at_z(d):
        return lax.rem(z + d, NZ)

    def dev_x(d):
        return (tile, at_x(d) * NZ + z)

    def dev_z(d):
        return (tile, x * NZ + at_z(d))

    place = tile * NX + x

    def dev_q(d):
        q = lax.rem(place + d + 32, 32)
        return (q // NX, lax.rem(q, NX) * NZ + z)

    loads = []
    for a in range(A_DEV):
        for b in range(BLOCKS):
            copy = pltpu.make_async_copy(
                stack_hbm.at[a, :, :, pl.ds(b * 128, 128)], stack.at[a, b], load_sem.at[a, b]
            )
            copy.start()
            loads.append(copy)

    barrier = pltpu.get_barrier_semaphore()
    partners = [dev_x(d) for d in range(1, NX)] + [dev_z(d) for d in range(1, NZ)] + [dev_q(1), dev_q(-1)]
    for partner in partners:
        pl.semaphore_signal(barrier, inc=1, device_id=partner, device_id_type=MESH)

    def send(src, dst, ssem, rsem, device):
        copy = pltpu.make_async_remote_copy(
            src_ref=src, dst_ref=dst, send_sem=ssem, recv_sem=rsem, device_id=device, device_id_type=MESH
        )
        copy.start()

    def wait(ref, sem):
        pltpu.make_async_copy(ref, ref, sem).wait()

    mine = [order[acq * A_DEV + a] for a in range(A_DEV)]
    ref_no = [refs[k] for k in range(NREF)]
    is_ref = []
    for a in range(A_DEV):
        hit = jnp.int32(0)
        for k in range(NREF):
            hit = hit + jnp.where(mine[a] == ref_no[k], 1, 0)
        is_ref.append(jnp.minimum(hit, 1))
    n_ref = is_ref[0] + is_ref[1] + is_ref[2] + is_ref[3]
    position, refs_before, others_before = [], jnp.int32(0), jnp.int32(0)
    for a in range(A_DEV):
        position.append(jnp.where(is_ref[a] > 0, refs_before, n_ref + others_before))
        refs_before = refs_before + is_ref[a]
        others_before = others_before + 1 - is_ref[a]
    local = []
    for c in range(A_DEV):
        where = jnp.int32(0)
        for a in range(A_DEV):
            where = where + jnp.where(position[a] == c, a, 0)
        local.append(jnp.minimum(where, A_DEV - 1))

    lane = lax.broadcasted_iota(jnp.int32, (CAP, 128), 1)
    sub = lax.broadcasted_iota(jnp.int32, (CAP, 128), 0)
    rows = jnp.zeros((CAP, 128), jnp.float32)
    facts = jnp.zeros((CAP, 128), jnp.int32)
    for s in range(CAP):
        kind, second = pairs[0, s], pairs[1, s]
        live = jnp.where(kind >= 0, 1, 0)
        kind = jnp.maximum(kind, 0)
        first = refs[kind]
        spot = jnp.int32(0)
        for a in range(A_DEV):
            spot = spot + jnp.where(mine[a] == second, a, 0)
        spot = jnp.minimum(spot, A_DEV - 1)
        row = jnp.where(lane == first, 1.0, 0.0) - jnp.where(lane == second, 1.0, 0.0)
        row = jnp.where(live > 0, row, 0.0)
        rows = jnp.where(sub == s, row, rows)
        fact = jnp.where(lane == 0, kind, jnp.where(lane == 1, spot, jnp.where(lane == 2, live, 0)))
        facts = jnp.where(sub == s, fact, facts)
    info[x] = facts
    da[z, x] = rows

    for copy in loads:
        copy.wait()

    def arrange(c):
        def body(t, carry):
            q, part = t // 2, lax.rem(t, 2)
            for j in range(LOOKS):
                for b in range(BLOCKS):
                    h, inner = divmod(b, BLOCKS // nc)
                    ps[c, q, h, part, j, :, pl.ds(inner * 128, 128)] = stack[
                        c, b, part, pl.ds(q * (ROWS * LOOKS) + j, ROWS, stride=LOOKS), :
                    ]
            return carry

        lax.fori_loop(0, NX * 2, body, 0)

    own = {}
    three, seven = pl.ds(0, NX - 1), pl.ds(0, NZ - 1)

    def send_chunk(c, h):
        for d in (1, 3, 2):
            send(ps.at[c, at_x(d), h], xg[h].at[c, x], s1s.at[c, h], s1r.at[c, h], dev_x(d))
        own[c, h] = pltpu.make_async_copy(ps.at[c, x, h], xg[h].at[c, x], own_sem.at[c, h])
        own[c, h].start()

    def sent(c, h):
        wait(ps.at[c, three, h], s1s.at[c, h])

    def arrived(c, h):
        wait(xg[h].at[c, three], s1r.at[c, h])
        own[c, h].wait()

    def scatter_fill():
        for r in range(chunks):
            def body(q, carry, r=r):
                for part in range(2):
                    for j in range(LOOKS):
                        for b in range(BLOCKS):
                            zs[part * LOOKS + j, r, q, :, pl.ds(b * 128, 128)] = stack[
                                local[r], b, part, pl.ds(q * (ROWS * LOOKS) + j, ROWS, stride=LOOKS), :
                            ]
                return carry

            lax.fori_loop(0, NX, body, 0)

    def scatter():
        for d in (4, 3, 5, 2, 6, 1, 7):
            send(zs.at[at_z(d)], zr.at[z], rs_s, rs_r, dev_z(d))
        zr[z] = zs[z]

    def find(n, slots):
        return tuple(slots[k] + jnp.where(order[n] == ref_no[k], n, 0) for k in range(NREF))

    def scatter_x(where_ref):
        wait(zr.at[seven], rs_r)
        for k in range(NREF):
            _, rz, rank = where_ref[k]
            for q in range(NX):
                yx[q, k] = zr[rz, rank, q]
        for d in (2, 1, 3):
            send(yx.at[at_x(d)], yr.at[x], y_s, y_r, dev_x(d))
        yr[x] = yx[x]

    half = NREF // 2
    halves = (pl.ds(0, half), pl.ds(half, half))

    def sign(way, d):
        return d if way == 0 else NZ - d

    def gather_first(h, where_ref):
        wait(yr.at[three], y_r)
        for k in range(NREF):
            rf[h][z, k] = yr[where_ref[k][0], k]
        for d in (2, 1):
            if d == 1:
                for way in range(2):
                    wait(rf[h].at[z], ag_s.at[h, way, 1])
            for way in range(2):
                send(
                    rf[h].at[z], rf[h].at[z], ag_s.at[h, way, d - 1], ag_r.at[h, way, d - 1], dev_z(sign(way, d))
                )

    def gather_second(h):
        for way in range(2):
            origin = at_z(sign(way, NZ - 2))
            wait(rf[h].at[origin], ag_r.at[h, way, 1])
            send(rf[h].at[origin], rf[h].at[origin], ag_s.at[h, way, 2], ag_r.at[h, way, 2], dev_z(sign(way, 1)))
            part = rf[h].at[origin, halves[way]]
            send(part, part, ag_s.at[h, way, 3], ag_r.at[h, way, 3], dev_z(sign(way, 2)))

    def gathered(h):
        for way in range(2):
            wait(rf[h].at[0], ag_r.at[h, way, 0])
            wait(rf[h].at[0], ag_r.at[h, way, 2])
            wait(rf[h].at[0, halves[way]], ag_r.at[h, way, 3])

    def solve():
        wait(da.at[seven], d2r.at[1])
        xt[...] = make_solver(da[...].reshape(NZ * NX * CAP, NACQ), ref_no)

    def facts_around():
        wait(info.at[three], ir)
        to_smem = pltpu.make_async_copy(info, info_s, i_sem)
        to_smem.start()
        wait(da.at[0, three], d2r.at[0])
        for d in range(1, NZ):
            send(da.at[z], da.at[z], d2s.at[1], d2r.at[1], dev_z(d))
        to_smem.wait()

    scatter_fill()
    pl.semaphore_wait(barrier, len(partners))
    scatter()
    for d in range(1, NX):
        send(info.at[x], info.at[x], is_, ir, dev_x(d))
        send(da.at[z, x], da.at[z, x], d2s.at[0], d2r.at[0], dev_x(d))
    for c in range(2):
        arrange(c)
        send_chunk(c, 0)
    for c in range(2, A_DEV):
        arrange(c)
    slots = lax.fori_loop(0, NACQ, find, (jnp.int32(0),) * NREF)
    slots = [jnp.minimum(slot, NACQ - 1) for slot in slots]
    owner = [lax.shift_right_logical(slot, 2) for slot in slots]
    where_ref = []
    for k in range(NREF):
        rank = jnp.int32(0)
        for other in range(NREF):
            if other != k:
                rank = rank + jnp.where((owner[other] == owner[k]) & (slots[other] < slots[k]), 1, 0)
        where_ref.append(
            (lax.shift_right_logical(owner[k], 3), lax.rem(owner[k], NZ), jnp.minimum(rank, chunks - 1))
        )
    facts_around()
    scatter_x(where_ref)
    wait(yx.at[three], y_s)
    for c in range(2, A_DEV):
        send_chunk(c, 0)
    gather_first(0, where_ref)
    gather_second(0)
    solve()

    def keep(q, v, columns):
        quant[q, :, columns] = v
        hlo[pl.ds(q, 1), columns] = v[0:1, :]
        hhi[pl.ds(q, 1), columns] = v[ROWS - 1 : ROWS, :]

    col = lax.broadcasted_iota(jnp.int32, (ROWS, COLS), 1)
    row = lax.broadcasted_iota(jnp.int32, (ROWS, COLS), 0)
    below = jnp.where(place > 0, 1.0, 0.0)
    above = jnp.where(place < 31, 1.0, 0.0)
    pairs_rows = 2 * CAP
    power_rows = pl.ds(2 * SLOTS, QPAD - 2 * SLOTS)

    def five(v):
        out = v
        for by in (1, 2):
            out = out + jnp.where(col >= by, pltpu.roll(v, by, 1), 0.0)
            out = out + jnp.where(col < COLS - by, pltpu.roll(v, COLS - by, 1), 0.0)
        return out

    def group_rows(group):
        return pl.ds(group * pairs_rows, pairs_rows)

    def send_halo(rows_, piece):
        send(hlo.at[rows_], rhi.at[rows_], h_s.at[0, piece], h_r.at[0, piece], dev_q(-1))
        send(hhi.at[rows_], rlo.at[rows_], h_s.at[1, piece], h_r.at[1, piece], dev_q(1))

    def halo_here(rows_, piece, count):
        wait(rhi.at[rows_], h_r.at[0, piece])
        wait(rlo.at[rows_], h_r.at[1, piece])
        for i in range(count // 8):
            block = pl.ds(rows_.start + 8 * i, 8)
            lo, hi = five(rlo[block, :]) * below, five(rhi[block, :]) * above
            rlo[block, :], rhi[block, :] = lo, hi

    def column_sums(start, count):
        def body(t, carry):
            values = [five(quant[start + 4 * t + i]) for i in range(4)]
            for i in range(4):
                quant[start + 4 * t + i] = values[i]
            return carry

        lax.fori_loop(0, count // 4, body, 0)

    def boxed(q):
        v = quant[q]
        down = jnp.where(row == 0, rlo[pl.ds(q, 1), :], pltpu.roll(v, 1, 0))
        up = jnp.where(row == ROWS - 1, rhi[pl.ds(q, 1), :], pltpu.roll(v, ROWS - 1, 0))
        return v + down + up

    for rest in (hlo, hhi):
        rest[QUANT:QPAD, :] = jnp.zeros((QPAD - QUANT, COLS), jnp.float32)
    gathered(0)
    for c in range(A_DEV):
        arrived(c, 0)
    full = pl.ds(0, COLS)
    for k in range(NREF):
        total = None
        for j in range(LOOKS):
            a, b = rf[0][j, k], rf[0][LOOKS + j, k]
            term = a * a + b * b
            total = term if j == 0 else total + term
        keep(2 * SLOTS + k, total, full)

    def power_body(s, carry):
        total = None
        for j in range(LOOKS):
            c, d = xg[0][lax.rem(s, A_DEV), s // A_DEV, 0, j], xg[0][lax.rem(s, A_DEV), s // A_DEV, 1, j]
            term = c * c + d * d
            total = term if j == 0 else total + term
        keep(2 * SLOTS + NREF + s, total, full)
        return carry

    order_d = (2, 1, 3, 0)
    for group in range(NX):

        def slot_body(index, carry, group=group):
            kind, spot, live = info_s[group, index, 0], info_s[group, index, 1], info_s[group, index, 2]
            real = imag = None
            for j in range(LOOKS):
                a, b = rf[0][j, kind], rf[0][LOOKS + j, kind]
                c, e = xg[0][spot, group, 0, j], xg[0][spot, group, 1, j]
                re, im = a * c + b * e, b * c - a * e
                real, imag = (re, im) if j == 0 else (real + re, imag + im)
            keep(group * pairs_rows + index, real, full)
            keep(group * pairs_rows + CAP + index, imag, full)
            phase = jnp.where(live > 0, atan2(imag, real), 0.0)
            for b in range(BLOCKS):
                ph[0, b, pl.ds(group * CAP + index, ROWS, stride=SLOTS), :] = phase[:, b * 128 : (b + 1) * 128]
            return carry

        lax.fori_loop(0, CAP, slot_body, 0)
        send_halo(group_rows(group), group)
    for d in range(1, NZ):
        target = at_z(d)
        block = pl.ds(pl.multiple_of(target * SLOTS, SLOTS), SLOTS)
        mine_there = pl.ds(pl.multiple_of(z * SLOTS, SLOTS), SLOTS)
        send(ph.at[0, :, block], pa.at[0, :, mine_there], pa_s.at[0], pa_r.at[0], dev_z(d))
    here = pl.ds(pl.multiple_of(z * SLOTS, SLOTS), SLOTS)
    pa[0, :, here] = ph[0, :, here]

    lax.fori_loop(0, ACQS, power_body, 0)
    send_halo(power_rows, NX)
    column_sums(0, QUANT)
    halo_here(power_rows, NX, QPAD - 2 * SLOTS)

    def power_box(t, carry):
        values = [boxed(2 * SLOTS + 4 * t + i) for i in range(4)]
        for i in range(4):
            quant[2 * SLOTS + 4 * t + i] = values[i]
        return carry

    lax.fori_loop(0, (NREF + ACQS) // 4, power_box, 0)
    for group in range(NX):
        halo_here(group_rows(group), group, pairs_rows)
    quarter = pl.ds(pl.multiple_of(x * ROWS, ROWS), ROWS)
    for d in order_d:
        group = at_x(d)

        def coherence_body(t, carry, group=group):
            values = []
            for i in range(2):
                index = 2 * t + i
                kind, spot, live = info_s[group, index, 0], info_s[group, index, 1], info_s[group, index, 2]
                real, imag = boxed(group * pairs_rows + index), boxed(group * pairs_rows + CAP + index)
                first = quant[2 * SLOTS + kind]
                second = quant[2 * SLOTS + NREF + group * A_DEV + spot]
                value = jnp.sqrt(real * real + imag * imag) / jnp.sqrt(first * second)
                values.append(jnp.where(live > 0, value, 0.0))
            for i in range(2):
                coh[group, 2 * t + i] = values[i]
            return carry

        lax.fori_loop(0, CAP // 2, coherence_body, 0)
        if d:
            send(coh.at[group], coherence.at[:, quarter, :], co_s, co_r, dev_x(d))
    coherence[:, quarter, :] = coh[x]

    for h in range(nc):
        wait(pa.at[h, :, pl.ds(0, (NZ - 1) * SLOTS)], pa_r.at[h])
        for b in range(BLOCKS // nc):
            series[pl.ds(h * width + b * 128, 128), :] = dot(pa[h, b], xt[...], ((0,), (0,)))

    wait(coh.at[three], co_r)
    wait(coh.at[three], co_s)
    wait(info.at[three], is_)
    wait(da.at[0, three], d2s.at[0])
    wait(da.at[seven], d2s.at[1])
    for h in range(nc):
        for c in range(A_DEV):
            sent(c, h)
        wait(zs.at[seven], rs_s)
        wait(pa.at[h, :, pl.ds(0, (NZ - 1) * SLOTS)], pa_s.at[h])
        for way in range(2):
            for step in (0, 2):
                wait(rf[h].at[0], ag_s.at[h, way, step])
            wait(rf[h].at[0, halves[way]], ag_s.at[h, way, 3])
        for way in range(2):
            wait(hlo.at[power_rows], h_s.at[way, NX])
            for group in range(NX):
                wait(hlo.at[pl.ds(0, pairs_rows)], h_s.at[way, group])


def call(chunks, nc, cid, stack, pairs, order, refs):
    width = COLS // nc
    f32 = jnp.float32
    dma = pltpu.SemaphoreType.DMA
    smem = pl.BlockSpec(memory_space=pltpu.SMEM)
    vmem = pl.BlockSpec(memory_space=pltpu.VMEM)
    return pl.pallas_call(
        functools.partial(kernel, chunks, nc),
        out_shape=(
            jax.ShapeDtypeStruct((COLS, NACQ), f32),
            jax.ShapeDtypeStruct((CAP, NX * ROWS, COLS), f32),
        ),
        in_specs=[pl.BlockSpec(memory_space=pl.ANY), smem, smem, smem],
        out_specs=(vmem, vmem),
        scratch_shapes=[
            pltpu.VMEM((A_DEV, BLOCKS, 2, NX * ROWS * LOOKS, 128), f32),
            pltpu.VMEM((A_DEV, NX, nc, 2, LOOKS, ROWS, width), f32),
            [pltpu.VMEM((A_DEV, NX, 2, LOOKS, ROWS, width), f32)] * nc,
            pltpu.VMEM((NZ, chunks, NX, ROWS, COLS), f32),
            pltpu.VMEM((NZ, chunks, NX, ROWS, COLS), f32),
            pltpu.VMEM((NX, NREF, ROWS, COLS), f32),
            pltpu.VMEM((NX, NREF, ROWS, COLS), f32),
            [pltpu.VMEM((NZ, NREF, ROWS, width), f32)] * nc,
            pltpu.VMEM((nc, BLOCKS // nc, ROWS * SLOTS, 128), f32),
            pltpu.VMEM((nc, BLOCKS // nc, NZ * SLOTS, 128), f32),
            pltpu.VMEM((NX, CAP, 128), jnp.int32),
            pltpu.SMEM((NX, CAP, 128), jnp.int32),
            pltpu.VMEM((NZ, NX, CAP, NACQ), f32),
            pltpu.VMEM((NZ * NX * CAP, NACQ), f32),
            pltpu.VMEM((QUANT, ROWS, COLS), f32),
            pltpu.VMEM((QPAD, COLS), f32),
            pltpu.VMEM((QPAD, COLS), f32),
            pltpu.VMEM((QPAD, COLS), f32),
            pltpu.VMEM((QPAD, COLS), f32),
            pltpu.VMEM((NX, CAP, ROWS, COLS), f32),
            dma((A_DEV, BLOCKS)), dma((A_DEV, nc)), dma((A_DEV, nc)), dma, dma, dma, dma((2,)), dma((2,)),
            dma, dma, dma, dma, dma((nc, 2, 4)), dma((nc, 2, 4)), dma((nc,)), dma((nc,)),
            dma((2, NX + 1)), dma((2, NX + 1)), dma, dma, dma((A_DEV, nc)),
        ],
        compiler_params=pltpu.CompilerParams(
            collective_id=cid, has_side_effects=True, vmem_limit_bytes=48 << 20
        ),
        name=f"sbas{chunks}",
    )(stack, pairs, order, refs)


def local(stack, pairs, order, refs):
    numbers = jnp.arange(NACQ, dtype=jnp.int32)
    slot = jnp.sum(jnp.where(order[None, :] == refs[:, None], numbers[None, :], 0), axis=1)
    owner = slot // A_DEV
    together = jnp.sum((owner[None, :] == owner[:, None]).astype(jnp.int32))
    pick = jnp.where(together > 8, 2, jnp.where(together > 4, 1, 0))
    variants = [functools.partial(call, 1, NC, 1), functools.partial(call, 2, NC, 2), functools.partial(call, 4, NC, 3)]
    return lax.switch(pick, variants, stack, pairs.T, order, refs)


NC = 1


def solution(mesh):
    return jax.shard_map(
        local,
        mesh=mesh,
        in_specs=(P("acq", None, "tile", None), P("acq", None), P(), P()),
        out_specs=(P(("tile", "acq"), None), P("acq", "tile", None)),
        check_vma=False,
    )
```

```python
import functools

import jax
import jax.numpy as jnp
from jax import lax
from jax.experimental import pallas as pl
from jax.experimental.pallas import tpu as pltpu
from jax.sharding import PartitionSpec as P

MESH = pl.DeviceIdType.MESH
HIGHEST = lax.Precision.HIGHEST
NREF = 4
LOOKS = 4
NX = 4
NZ = 8
A_DEV = 4
CAP = 8
COLS = 512
BLOCKS = 4
ROWS = 8
NACQ = 128
SLOTS = NX * CAP
ACQS = NX * A_DEV
QUANT = 2 * SLOTS + NREF + ACQS
QPAD = 88

ATAN = (
    1.0, -0.33333277702331543, 0.1999807506799698, -0.1426001638174057, 0.1093234121799469,
    -0.08349724858999252, 0.05708955600857735, -0.03035186603665352, 0.010487649589776993,
    -0.0017011701129376888,
)


def atan2(y, x):
    ax, ay = jnp.abs(x), jnp.abs(y)
    t = jnp.minimum(ax, ay) / jnp.maximum(ax, ay)
    u = t * t
    acc = jnp.full_like(u, ATAN[-1])
    for coefficient in ATAN[-2::-1]:
        acc = acc * u + coefficient
    r = acc * t
    r = jnp.where(ay > ax, jnp.pi / 2 - r, r)
    r = jnp.where(x < 0, jnp.pi - r, r)
    return jnp.where(y < 0, -r, r)


def dot(a, b, dims):
    return lax.dot_general(a, b, (dims, ((), ())), precision=HIGHEST, preferred_element_type=jnp.float32)


def make_solver(design, refs):
    lane = lax.broadcasted_iota(jnp.int32, (8, NACQ), 1)
    sub = lax.broadcasted_iota(jnp.int32, (8, NACQ), 0)
    pick = jnp.zeros((8, NACQ), jnp.float32)
    for k in range(NREF):
        pick = jnp.where((sub == k) & (lane == refs[k]), 1.0, pick)
    is_ref = jnp.sum(pick, axis=0, keepdims=True)
    other = 1.0 - is_ref
    degree = jnp.sum(design * design, axis=0, keepdims=True)
    inverse = other / (1.0 + degree)
    on_ref = dot(design, pick, ((1,), (1,)))
    normal_ref = dot(on_ref, design, ((0,), (0,))) + pick
    right = on_ref - dot(design * inverse, normal_ref, ((1,), (1,)))
    schur = dot(normal_ref, pick, ((1,), (1,))) - dot(normal_ref * inverse, normal_ref, ((1,), (1,)))
    row8 = lax.broadcasted_iota(jnp.int32, (8, 8), 0)
    col8 = lax.broadcasted_iota(jnp.int32, (8, 8), 1)
    eye8 = jnp.where(row8 == col8, 1.0, 0.0)
    left = schur + jnp.where(row8 >= NREF, eye8, 0.0)
    inv = eye8
    for k in range(NREF):
        pivot = 1.0 / left[k : k + 1, k : k + 1]
        lrow, irow = left[k : k + 1, :] * pivot, inv[k : k + 1, :] * pivot
        column = jnp.where(row8[:, 0:1] == k, 0.0, left[:, k : k + 1])
        left = jnp.where(row8 == k, lrow, left - column * lrow)
        inv = jnp.where(row8 == k, irow, inv - column * irow)
    at_ref = dot(right, inv, ((1,), (0,)))
    rest = (design - dot(at_ref, normal_ref, ((1,), (0,)))) * inverse
    return rest + dot(at_ref, pick, ((1,), (0,)))


def kernel(
    chunks, nc,
    stack_hbm, pairs, order, refs, series, coherence,
    stack, ps, xg, zs, zr, yx, yr, rf, ph, pa, info, info_s, da, xt, quant, hlo, hhi, rlo, rhi, coh,
    load_sem, s1s, s1r, i_sem, is_, ir, d2s, d2r, rs_s, rs_r, y_s, y_r, ag_s, ag_r, pa_s, pa_r, h_s, h_r, co_s, co_r, own_sem,
):
    width = COLS // nc
    tile, acq = lax.axis_index("tile"), lax.axis_index("acq")
    x, z = acq // NZ, lax.rem(acq, NZ)

    def at_x(d):
        return lax.rem(x + d, NX)

    def at_z(d):
        return lax.rem(z + d, NZ)

    def dev_x(d):
        return (tile, at_x(d) * NZ + z)

    def dev_z(d):
        return (tile, x * NZ + at_z(d))

    place = tile * NX + x

    def dev_q(d):
        q = lax.rem(place + d + 32, 32)
        return (q // NX, lax.rem(q, NX) * NZ + z)

    loads = []
    for a in range(A_DEV):
        for b in range(BLOCKS):
            copy = pltpu.make_async_copy(
                stack_hbm.at[a, :, :, pl.ds(b * 128, 128)], stack.at[a, b], load_sem.at[a, b]
            )
            copy.start()
            loads.append(copy)

    barrier = pltpu.get_barrier_semaphore()
    partners = [dev_x(d) for d in range(1, NX)] + [dev_z(d) for d in range(1, NZ)] + [dev_q(1), dev_q(-1)]
    for partner in partners:
        pl.semaphore_signal(barrier, inc=1, device_id=partner, device_id_type=MESH)

    def send(src, dst, ssem, rsem, device):
        copy = pltpu.make_async_remote_copy(
            src_ref=src, dst_ref=dst, send_sem=ssem, recv_sem=rsem, device_id=device, device_id_type=MESH
        )
        copy.start()

    def wait(ref, sem):
        pltpu.make_async_copy(ref, ref, sem).wait()

    mine = [order[acq * A_DEV + a] for a in range(A_DEV)]
    ref_no = [refs[k] for k in range(NREF)]
    is_ref = []
    for a in range(A_DEV):
        hit = jnp.int32(0)
        for k in range(NREF):
            hit = hit + jnp.where(mine[a] == ref_no[k], 1, 0)
        is_ref.append(jnp.minimum(hit, 1))
    n_ref = is_ref[0] + is_ref[1] + is_ref[2] + is_ref[3]
    position, refs_before, others_before = [], jnp.int32(0), jnp.int32(0)
    for a in range(A_DEV):
        position.append(jnp.where(is_ref[a] > 0, refs_before, n_ref + others_before))
        refs_before = refs_before + is_ref[a]
        others_before = others_before + 1 - is_ref[a]
    local = []
    for c in range(A_DEV):
        where = jnp.int32(0)
        for a in range(A_DEV):
            where = where + jnp.where(position[a] == c, a, 0)
        local.append(jnp.minimum(where, A_DEV - 1))

    lane = lax.broadcasted_iota(jnp.int32, (CAP, 128), 1)
    sub = lax.broadcasted_iota(jnp.int32, (CAP, 128), 0)
    rows = jnp.zeros((CAP, 128), jnp.float32)
    facts = jnp.zeros((CAP, 128), jnp.int32)
    for s in range(CAP):
        kind, second = pairs[0, s], pairs[1, s]
        live = jnp.where(kind >= 0, 1, 0)
        kind = jnp.maximum(kind, 0)
        first = refs[kind]
        spot = jnp.int32(0)
        for a in range(A_DEV):
            spot = spot + jnp.where(mine[a] == second, a, 0)
        spot = jnp.minimum(spot, A_DEV - 1)
        row = jnp.where(lane == first, 1.0, 0.0) - jnp.where(lane == second, 1.0, 0.0)
        row = jnp.where(live > 0, row, 0.0)
        rows = jnp.where(sub == s, row, rows)
        fact = jnp.where(lane == 0, kind, jnp.where(lane == 1, spot, jnp.where(lane == 2, live, 0)))
        facts = jnp.where(sub == s, fact, facts)
    info[x] = facts
    da[z, x] = rows

    for copy in loads:
        copy.wait()

    def arrange(c):
        def body(t, carry):
            q, part = t // 2, lax.rem(t, 2)
            for j in range(LOOKS):
                for b in range(BLOCKS):
                    h, inner = divmod(b, BLOCKS // nc)
                    ps[c, q, h, part, j, :, pl.ds(inner * 128, 128)] = stack[
                        c, b, part, pl.ds(q * (ROWS * LOOKS) + j, ROWS, stride=LOOKS), :
                    ]
            return carry

        lax.fori_loop(0, NX * 2, body, 0)

    own = {}
    three, seven = pl.ds(0, NX - 1), pl.ds(0, NZ - 1)

    def send_chunk(c, h):
        for d in (1, 3, 2):
            send(ps.at[c, at_x(d), h], xg[h].at[c, x], s1s.at[c, h], s1r.at[c, h], dev_x(d))
        own[c, h] = pltpu.make_async_copy(ps.at[c, x, h], xg[h].at[c, x], own_sem.at[c, h])
        own[c, h].start()

    def sent(c, h):
        wait(ps.at[c, three, h], s1s.at[c, h])

    def arrived(c, h):
        wait(xg[h].at[c, three], s1r.at[c, h])
        own[c, h].wait()

    def scatter_fill():
        for r in range(chunks):
            def body(q, carry, r=r):
                for part in range(2):
                    for j in range(LOOKS):
                        for b in range(BLOCKS):
                            zs[part * LOOKS + j, r, q, :, pl.ds(b * 128, 128)] = stack[
                                local[r], b, part, pl.ds(q * (ROWS * LOOKS) + j, ROWS, stride=LOOKS), :
                            ]
                return carry

            lax.fori_loop(0, NX, body, 0)

    def scatter():
        for d in (4, 3, 5, 2, 6, 1, 7):
            send(zs.at[at_z(d)], zr.at[z], rs_s, rs_r, dev_z(d))
        zr[z] = zs[z]

    def find(n, slots):
        return tuple(slots[k] + jnp.where(order[n] == ref_no[k], n, 0) for k in range(NREF))

    def scatter_x(where_ref):
        wait(zr.at[seven], rs_r)
        for k in range(NREF):
            _, rz, rank = where_ref[k]
            for q in range(NX):
                yx[q, k] = zr[rz, rank, q]
        for d in (2, 1, 3):
            send(yx.at[at_x(d)], yr.at[x], y_s, y_r, dev_x(d))
        yr[x] = yx[x]

    half = NREF // 2
    halves = (pl.ds(0, half), pl.ds(half, half))

    def sign(way, d):
        return d if way == 0 else NZ - d

    def gather_first(h, where_ref):
        wait(yr.at[three], y_r)
        for k in range(NREF):
            rf[h][z, k] = yr[where_ref[k][0], k]
        for d in (2, 1):
            if d == 1:
                for way in range(2):
                    wait(rf[h].at[z], ag_s.at[h, way, 1])
            for way in range(2):
                send(
                    rf[h].at[z], rf[h].at[z], ag_s.at[h, way, d - 1], ag_r.at[h, way, d - 1], dev_z(sign(way, d))
                )

    def gather_second(h):
        for way in range(2):
            origin = at_z(sign(way, NZ - 2))
            wait(rf[h].at[origin], ag_r.at[h, way, 1])
            send(rf[h].at[origin], rf[h].at[origin], ag_s.at[h, way, 2], ag_r.at[h, way, 2], dev_z(sign(way, 1)))
            part = rf[h].at[origin, halves[way]]
            send(part, part, ag_s.at[h, way, 3], ag_r.at[h, way, 3], dev_z(sign(way, 2)))

    def gathered(h):
        for way in range(2):
            wait(rf[h].at[0], ag_r.at[h, way, 0])
            wait(rf[h].at[0], ag_r.at[h, way, 2])
            wait(rf[h].at[0, halves[way]], ag_r.at[h, way, 3])

    def solve():
        wait(da.at[seven], d2r.at[1])
        xt[...] = make_solver(da[...].reshape(NZ * NX * CAP, NACQ), ref_no)

    def facts_around():
        wait(info.at[three], ir)
        to_smem = pltpu.make_async_copy(info, info_s, i_sem)
        to_smem.start()
        wait(da.at[0, three], d2r.at[0])
        for d in range(1, NZ):
            send(da.at[z], da.at[z], d2s.at[1], d2r.at[1], dev_z(d))
        to_smem.wait()

    scatter_fill()
    pl.semaphore_wait(barrier, len(partners))
    scatter()
    for d in range(1, NX):
        send(info.at[x], info.at[x], is_, ir, dev_x(d))
        send(da.at[z, x], da.at[z, x], d2s.at[0], d2r.at[0], dev_x(d))
    for c in range(2):
        arrange(c)
        send_chunk(c, 0)
    for c in range(2, A_DEV):
        arrange(c)
    slots = lax.fori_loop(0, NACQ, find, (jnp.int32(0),) * NREF)
    slots = [jnp.minimum(slot, NACQ - 1) for slot in slots]
    owner = [lax.shift_right_logical(slot, 2) for slot in slots]
    where_ref = []
    for k in range(NREF):
        rank = jnp.int32(0)
        for other in range(NREF):
            if other != k:
                rank = rank + jnp.where((owner[other] == owner[k]) & (slots[other] < slots[k]), 1, 0)
        where_ref.append(
            (lax.shift_right_logical(owner[k], 3), lax.rem(owner[k], NZ), jnp.minimum(rank, chunks - 1))
        )
    scatter_x(where_ref)
    facts_around()
    wait(yx.at[three], y_s)
    for c in range(2, A_DEV):
        send_chunk(c, 0)
    gather_first(0, where_ref)
    gather_second(0)
    solve()

    def keep(q, v, columns):
        quant[q, :, columns] = v
        hlo[pl.ds(q, 1), columns] = v[0:1, :]
        hhi[pl.ds(q, 1), columns] = v[ROWS - 1 : ROWS, :]

    col = lax.broadcasted_iota(jnp.int32, (ROWS, COLS), 1)
    row = lax.broadcasted_iota(jnp.int32, (ROWS, COLS), 0)
    below = jnp.where(place > 0, 1.0, 0.0)
    above = jnp.where(place < 31, 1.0, 0.0)
    pairs_rows = 2 * CAP
    power_rows = pl.ds(2 * SLOTS, QPAD - 2 * SLOTS)

    def five(v):
        out = v
        for by in (1, 2):
            out = out + jnp.where(col >= by, pltpu.roll(v, by, 1), 0.0)
            out = out + jnp.where(col < COLS - by, pltpu.roll(v, COLS - by, 1), 0.0)
        return out

    def group_rows(group):
        return pl.ds(group * pairs_rows, pairs_rows)

    def send_halo(rows_, piece):
        send(hlo.at[rows_], rhi.at[rows_], h_s.at[0, piece], h_r.at[0, piece], dev_q(-1))
        send(hhi.at[rows_], rlo.at[rows_], h_s.at[1, piece], h_r.at[1, piece], dev_q(1))

    def halo_here(rows_, piece, count):
        wait(rhi.at[rows_], h_r.at[0, piece])
        wait(rlo.at[rows_], h_r.at[1, piece])
        for i in range(count // 8):
            block = pl.ds(rows_.start + 8 * i, 8)
            lo, hi = five(rlo[block, :]) * below, five(rhi[block, :]) * above
            rlo[block, :], rhi[block, :] = lo, hi

    def column_sums(start, count):
        def body(t, carry):
            values = [five(quant[start + 4 * t + i]) for i in range(4)]
            for i in range(4):
                quant[start + 4 * t + i] = values[i]
            return carry

        lax.fori_loop(0, count // 4, body, 0)

    def boxed(q):
        v = quant[q]
        down = jnp.where(row == 0, rlo[pl.ds(q, 1), :], pltpu.roll(v, 1, 0))
        up = jnp.where(row == ROWS - 1, rhi[pl.ds(q, 1), :], pltpu.roll(v, ROWS - 1, 0))
        return v + down + up

    for rest in (hlo, hhi):
        rest[QUANT:QPAD, :] = jnp.zeros((QPAD - QUANT, COLS), jnp.float32)
    gathered(0)
    for c in range(A_DEV):
        arrived(c, 0)
    full = pl.ds(0, COLS)
    for k in range(NREF):
        total = None
        for j in range(LOOKS):
            a, b = rf[0][j, k], rf[0][LOOKS + j, k]
            term = a * a + b * b
            total = term if j == 0 else total + term
        keep(2 * SLOTS + k, total, full)

    def power_body(s, carry):
        total = None
        for j in range(LOOKS):
            c, d = xg[0][lax.rem(s, A_DEV), s // A_DEV, 0, j], xg[0][lax.rem(s, A_DEV), s // A_DEV, 1, j]
            term = c * c + d * d
            total = term if j == 0 else total + term
        keep(2 * SLOTS + NREF + s, total, full)
        return carry

    def send_phases(part):
        here = pl.ds(pl.multiple_of(z * pairs_rows, pairs_rows), pairs_rows)
        for d in (4, 3, 5, 2, 6, 1, 7):
            block = pl.ds(pl.multiple_of(at_z(d) * pairs_rows, pairs_rows), pairs_rows)
            send(ph.at[part, :, block], pa.at[part, :, here], pa_s.at[part], pa_r.at[part], dev_z(d))
        pa[part, :, here] = ph[part, :, here]

    order_d = (2, 1, 3, 0)
    for group in range(NX):

        def slot_body(index, carry, group=group):
            kind, spot, live = info_s[group, index, 0], info_s[group, index, 1], info_s[group, index, 2]
            real = imag = None
            for j in range(LOOKS):
                a, b = rf[0][j, kind], rf[0][LOOKS + j, kind]
                c, e = xg[0][spot, group, 0, j], xg[0][spot, group, 1, j]
                re, im = a * c + b * e, b * c - a * e
                real, imag = (re, im) if j == 0 else (real + re, imag + im)
            keep(group * pairs_rows + index, real, full)
            keep(group * pairs_rows + CAP + index, imag, full)
            phase = jnp.where(live > 0, atan2(imag, real), 0.0)
            for b in range(BLOCKS):
                ph[group // 2, b, pl.ds(group % 2 * CAP + index, ROWS, stride=pairs_rows), :] = phase[
                    :, b * 128 : (b + 1) * 128
                ]
            return carry

        lax.fori_loop(0, CAP, slot_body, 0)
        send_halo(group_rows(group), group)
        if group % 2 == 1:
            send_phases(group // 2)

    lax.fori_loop(0, ACQS, power_body, 0)
    send_halo(power_rows, NX)
    column_sums(2 * SLOTS, NREF + ACQS)
    column_sums(at_x(order_d[0]) * pairs_rows, pairs_rows)
    halo_here(power_rows, NX, QPAD - 2 * SLOTS)

    def power_box(t, carry):
        values = [boxed(2 * SLOTS + 4 * t + i) for i in range(4)]
        for i in range(4):
            quant[2 * SLOTS + 4 * t + i] = values[i]
        return carry

    lax.fori_loop(0, (NREF + ACQS) // 4, power_box, 0)
    for group in range(NX):
        halo_here(group_rows(group), group, pairs_rows)
    quarter = pl.ds(pl.multiple_of(x * ROWS, ROWS), ROWS)
    for d in order_d:
        group = at_x(d)
        if d != order_d[0]:
            column_sums(group * pairs_rows, pairs_rows)

        def coherence_body(t, carry, group=group):
            values = []
            for i in range(2):
                index = 2 * t + i
                kind, spot, live = info_s[group, index, 0], info_s[group, index, 1], info_s[group, index, 2]
                real, imag = boxed(group * pairs_rows + index), boxed(group * pairs_rows + CAP + index)
                first = quant[2 * SLOTS + kind]
                second = quant[2 * SLOTS + NREF + group * A_DEV + spot]
                value = jnp.sqrt(real * real + imag * imag) / jnp.sqrt(first * second)
                values.append(jnp.where(live > 0, value, 0.0))
            for i in range(2):
                coh[group, 2 * t + i] = values[i]
            return carry

        lax.fori_loop(0, CAP // 2, coherence_body, 0)
        if d:
            send(coh.at[group], coherence.at[:, quarter, :], co_s, co_r, dev_x(d))
    coherence[:, quarter, :] = coh[x]

    arrivals = pl.ds(0, (NZ - 1) * pairs_rows)
    for part in range(2):
        wait(pa.at[part, :, arrivals], pa_r.at[part])
        weights = xt[...].reshape(NZ, SLOTS, NACQ)[:, part * pairs_rows : (part + 1) * pairs_rows]
        weights = weights.reshape(NZ * pairs_rows, NACQ)
        for b in range(BLOCKS):
            rows_b = pl.ds(b * 128, 128)
            term = dot(pa[part, b], weights, ((0,), (0,)))
            series[rows_b, :] = term if part == 0 else series[rows_b, :] + term

    wait(coh.at[three], co_r)
    wait(coh.at[three], co_s)
    wait(info.at[three], is_)
    wait(da.at[0, three], d2s.at[0])
    wait(da.at[seven], d2s.at[1])
    for h in range(nc):
        for c in range(A_DEV):
            sent(c, h)
        wait(zs.at[seven], rs_s)
        for part in range(2):
            wait(pa.at[part, :, arrivals], pa_s.at[part])
        for way in range(2):
            for step in (0, 2):
                wait(rf[h].at[0], ag_s.at[h, way, step])
            wait(rf[h].at[0, halves[way]], ag_s.at[h, way, 3])
        for way in range(2):
            wait(hlo.at[power_rows], h_s.at[way, NX])
            for group in range(NX):
                wait(hlo.at[pl.ds(0, pairs_rows)], h_s.at[way, group])


def call(chunks, nc, cid, stack, pairs, order, refs):
    width = COLS // nc
    f32 = jnp.float32
    dma = pltpu.SemaphoreType.DMA
    smem = pl.BlockSpec(memory_space=pltpu.SMEM)
    vmem = pl.BlockSpec(memory_space=pltpu.VMEM)
    return pl.pallas_call(
        functools.partial(kernel, chunks, nc),
        out_shape=(
            jax.ShapeDtypeStruct((COLS, NACQ), f32),
            jax.ShapeDtypeStruct((CAP, NX * ROWS, COLS), f32),
        ),
        in_specs=[pl.BlockSpec(memory_space=pl.ANY), smem, smem, smem],
        out_specs=(vmem, vmem),
        scratch_shapes=[
            pltpu.VMEM((A_DEV, BLOCKS, 2, NX * ROWS * LOOKS, 128), f32),
            pltpu.VMEM((A_DEV, NX, nc, 2, LOOKS, ROWS, width), f32),
            [pltpu.VMEM((A_DEV, NX, 2, LOOKS, ROWS, width), f32)] * nc,
            pltpu.VMEM((NZ, chunks, NX, ROWS, COLS), f32),
            pltpu.VMEM((NZ, chunks, NX, ROWS, COLS), f32),
            pltpu.VMEM((NX, NREF, ROWS, COLS), f32),
            pltpu.VMEM((NX, NREF, ROWS, COLS), f32),
            [pltpu.VMEM((NZ, NREF, ROWS, width), f32)] * nc,
            pltpu.VMEM((2, BLOCKS, ROWS * SLOTS // 2, 128), f32),
            pltpu.VMEM((2, BLOCKS, NZ * SLOTS // 2, 128), f32),
            pltpu.VMEM((NX, CAP, 128), jnp.int32),
            pltpu.SMEM((NX, CAP, 128), jnp.int32),
            pltpu.VMEM((NZ, NX, CAP, NACQ), f32),
            pltpu.VMEM((NZ * NX * CAP, NACQ), f32),
            pltpu.VMEM((QUANT, ROWS, COLS), f32),
            pltpu.VMEM((QPAD, COLS), f32),
            pltpu.VMEM((QPAD, COLS), f32),
            pltpu.VMEM((QPAD, COLS), f32),
            pltpu.VMEM((QPAD, COLS), f32),
            pltpu.VMEM((NX, CAP, ROWS, COLS), f32),
            dma((A_DEV, BLOCKS)), dma((A_DEV, nc)), dma((A_DEV, nc)), dma, dma, dma, dma((2,)), dma((2,)),
            dma, dma, dma, dma, dma((nc, 2, 4)), dma((nc, 2, 4)), dma((2,)), dma((2,)),
            dma((2, NX + 1)), dma((2, NX + 1)), dma, dma, dma((A_DEV, nc)),
        ],
        compiler_params=pltpu.CompilerParams(
            collective_id=cid, has_side_effects=True, vmem_limit_bytes=48 << 20
        ),
        name=f"sbas{chunks}",
    )(stack, pairs, order, refs)


def local(stack, pairs, order, refs):
    numbers = jnp.arange(NACQ, dtype=jnp.int32)
    slot = jnp.sum(jnp.where(order[None, :] == refs[:, None], numbers[None, :], 0), axis=1)
    owner = slot // A_DEV
    together = jnp.sum((owner[None, :] == owner[:, None]).astype(jnp.int32))
    pick = jnp.where(together > 8, 2, jnp.where(together > 4, 1, 0))
    variants = [functools.partial(call, 1, NC, 1), functools.partial(call, 2, NC, 2), functools.partial(call, 4, NC, 3)]
    return lax.switch(pick, variants, stack, pairs.T, order, refs)


NC = 1


def solution(mesh):
    return jax.shard_map(
        local,
        mesh=mesh,
        in_specs=(P("acq", None, "tile", None), P("acq", None), P(), P()),
        out_specs=(P(("tile", "acq"), None), P("acq", "tile", None)),
        check_vma=False,
    )
```

```python
import functools

import jax
import jax.numpy as jnp
from jax import lax
from jax.experimental import pallas as pl
from jax.experimental.pallas import tpu as pltpu
from jax.sharding import PartitionSpec as P

MESH = pl.DeviceIdType.MESH
HIGHEST = lax.Precision.HIGHEST
NREF = 4
LOOKS = 4
NX = 4
NZ = 8
A_DEV = 4
CAP = 8
COLS = 512
BLOCKS = 4
ROWS = 8
NACQ = 128
SLOTS = NX * CAP
ACQS = NX * A_DEV
QUANT = 2 * SLOTS + NREF + ACQS
QPAD = 88

ATAN = (
    1.0, -0.33333277702331543, 0.1999807506799698, -0.1426001638174057, 0.1093234121799469,
    -0.08349724858999252, 0.05708955600857735, -0.03035186603665352, 0.010487649589776993,
    -0.0017011701129376888,
)


def atan2(y, x):
    ax, ay = jnp.abs(x), jnp.abs(y)
    t = jnp.minimum(ax, ay) / jnp.maximum(ax, ay)
    u = t * t
    acc = jnp.full_like(u, ATAN[-1])
    for coefficient in ATAN[-2::-1]:
        acc = acc * u + coefficient
    r = acc * t
    r = jnp.where(ay > ax, jnp.pi / 2 - r, r)
    r = jnp.where(x < 0, jnp.pi - r, r)
    return jnp.where(y < 0, -r, r)


def dot(a, b, dims):
    return lax.dot_general(a, b, (dims, ((), ())), precision=HIGHEST, preferred_element_type=jnp.float32)


def make_solver(design, refs):
    lane = lax.broadcasted_iota(jnp.int32, (8, NACQ), 1)
    sub = lax.broadcasted_iota(jnp.int32, (8, NACQ), 0)
    pick = jnp.zeros((8, NACQ), jnp.float32)
    for k in range(NREF):
        pick = jnp.where((sub == k) & (lane == refs[k]), 1.0, pick)
    is_ref = jnp.sum(pick, axis=0, keepdims=True)
    other = 1.0 - is_ref
    degree = jnp.sum(design * design, axis=0, keepdims=True)
    inverse = other / (1.0 + degree)
    on_ref = dot(design, pick, ((1,), (1,)))
    normal_ref = dot(on_ref, design, ((0,), (0,))) + pick
    right = on_ref - dot(design * inverse, normal_ref, ((1,), (1,)))
    schur = dot(normal_ref, pick, ((1,), (1,))) - dot(normal_ref * inverse, normal_ref, ((1,), (1,)))
    row8 = lax.broadcasted_iota(jnp.int32, (8, 8), 0)
    col8 = lax.broadcasted_iota(jnp.int32, (8, 8), 1)
    eye8 = jnp.where(row8 == col8, 1.0, 0.0)
    left = schur + jnp.where(row8 >= NREF, eye8, 0.0)
    inv = eye8
    for k in range(NREF):
        pivot = 1.0 / left[k : k + 1, k : k + 1]
        lrow, irow = left[k : k + 1, :] * pivot, inv[k : k + 1, :] * pivot
        column = jnp.where(row8[:, 0:1] == k, 0.0, left[:, k : k + 1])
        left = jnp.where(row8 == k, lrow, left - column * lrow)
        inv = jnp.where(row8 == k, irow, inv - column * irow)
    at_ref = dot(right, inv, ((1,), (0,)))
    rest = (design - dot(at_ref, normal_ref, ((1,), (0,)))) * inverse
    return rest + dot(at_ref, pick, ((1,), (0,)))


def kernel(
    chunks, nc,
    stack_hbm, pairs, order, refs, series, coherence,
    stack, ps, xg, zs, zr, yx, yr, rf, ph, pa, info, info_s, da, xt, quant, hlo, hhi, rlo, rhi, coh,
    load_sem, s1s, s1r, i_sem, is_, ir, d2s, d2r, rs_s, rs_r, y_s, y_r, ag_s, ag_r, pa_s, pa_r, h_s, h_r, co_s, co_r, own_sem,
):
    width = COLS // nc
    tile, acq = lax.axis_index("tile"), lax.axis_index("acq")
    x, z = acq // NZ, lax.rem(acq, NZ)

    def at_x(d):
        return lax.rem(x + d, NX)

    def at_z(d):
        return lax.rem(z + d, NZ)

    def dev_x(d):
        return (tile, at_x(d) * NZ + z)

    def dev_z(d):
        return (tile, x * NZ + at_z(d))

    place = tile * NX + x

    def dev_q(d):
        q = lax.rem(place + d + 32, 32)
        return (q // NX, lax.rem(q, NX) * NZ + z)

    loads = []
    for a in range(A_DEV):
        for b in range(BLOCKS):
            copy = pltpu.make_async_copy(
                stack_hbm.at[a, :, :, pl.ds(b * 128, 128)], stack.at[a, b], load_sem.at[a, b]
            )
            copy.start()
            loads.append(copy)

    barrier = pltpu.get_barrier_semaphore()
    partners = [dev_x(d) for d in range(1, NX)] + [dev_z(d) for d in range(1, NZ)] + [dev_q(1), dev_q(-1)]
    for partner in partners:
        pl.semaphore_signal(barrier, inc=1, device_id=partner, device_id_type=MESH)

    def send(src, dst, ssem, rsem, device):
        copy = pltpu.make_async_remote_copy(
            src_ref=src, dst_ref=dst, send_sem=ssem, recv_sem=rsem, device_id=device, device_id_type=MESH
        )
        copy.start()

    def wait(ref, sem):
        pltpu.make_async_copy(ref, ref, sem).wait()

    mine = [order[acq * A_DEV + a] for a in range(A_DEV)]
    ref_no = [refs[k] for k in range(NREF)]
    is_ref = []
    for a in range(A_DEV):
        hit = jnp.int32(0)
        for k in range(NREF):
            hit = hit + jnp.where(mine[a] == ref_no[k], 1, 0)
        is_ref.append(jnp.minimum(hit, 1))
    n_ref = is_ref[0] + is_ref[1] + is_ref[2] + is_ref[3]
    position, refs_before, others_before = [], jnp.int32(0), jnp.int32(0)
    for a in range(A_DEV):
        position.append(jnp.where(is_ref[a] > 0, refs_before, n_ref + others_before))
        refs_before = refs_before + is_ref[a]
        others_before = others_before + 1 - is_ref[a]
    local = []
    for c in range(A_DEV):
        where = jnp.int32(0)
        for a in range(A_DEV):
            where = where + jnp.where(position[a] == c, a, 0)
        local.append(jnp.minimum(where, A_DEV - 1))

    lane = lax.broadcasted_iota(jnp.int32, (CAP, 128), 1)
    sub = lax.broadcasted_iota(jnp.int32, (CAP, 128), 0)
    rows = jnp.zeros((CAP, 128), jnp.float32)
    facts = jnp.zeros((CAP, 128), jnp.int32)
    for s in range(CAP):
        kind, second = pairs[0, s], pairs[1, s]
        live = jnp.where(kind >= 0, 1, 0)
        kind = jnp.maximum(kind, 0)
        first = refs[kind]
        spot = jnp.int32(0)
        for a in range(A_DEV):
            spot = spot + jnp.where(mine[a] == second, a, 0)
        spot = jnp.minimum(spot, A_DEV - 1)
        row = jnp.where(lane == first, 1.0, 0.0) - jnp.where(lane == second, 1.0, 0.0)
        row = jnp.where(live > 0, row, 0.0)
        rows = jnp.where(sub == s, row, rows)
        fact = jnp.where(lane == 0, kind, jnp.where(lane == 1, spot, jnp.where(lane == 2, live, 0)))
        facts = jnp.where(sub == s, fact, facts)
    info[x] = facts
    da[z, x] = rows

    for copy in loads:
        copy.wait()

    def arrange(c):
        def body(t, carry):
            q, part = t // 2, lax.rem(t, 2)
            for j in range(LOOKS):
                for b in range(BLOCKS):
                    h, inner = divmod(b, BLOCKS // nc)
                    ps[c, q, h, part, j, :, pl.ds(inner * 128, 128)] = stack[
                        c, b, part, pl.ds(q * (ROWS * LOOKS) + j, ROWS, stride=LOOKS), :
                    ]
            return carry

        lax.fori_loop(0, NX * 2, body, 0)

    own = {}
    three, seven = pl.ds(0, NX - 1), pl.ds(0, NZ - 1)

    def send_chunk(c, h):
        for d in (1, 3, 2):
            send(ps.at[c, at_x(d), h], xg[h].at[c, x], s1s.at[c, h], s1r.at[c, h], dev_x(d))
        own[c, h] = pltpu.make_async_copy(ps.at[c, x, h], xg[h].at[c, x], own_sem.at[c, h])
        own[c, h].start()

    def sent(c, h):
        wait(ps.at[c, three, h], s1s.at[c, h])

    def arrived(c, h):
        wait(xg[h].at[c, three], s1r.at[c, h])
        own[c, h].wait()

    def scatter_fill():
        for r in range(chunks):
            def body(q, carry, r=r):
                for part in range(2):
                    for j in range(LOOKS):
                        for b in range(BLOCKS):
                            zs[part * LOOKS + j, r, q, :, pl.ds(b * 128, 128)] = stack[
                                local[r], b, part, pl.ds(q * (ROWS * LOOKS) + j, ROWS, stride=LOOKS), :
                            ]
                return carry

            lax.fori_loop(0, NX, body, 0)

    def scatter():
        for d in (4, 5, 3, 6, 2, 7, 1):
            send(zs.at[at_z(d)], zr.at[z], rs_s, rs_r, dev_z(d))
        zr[z] = zs[z]

    def find(n, slots):
        return tuple(slots[k] + jnp.where(order[n] == ref_no[k], n, 0) for k in range(NREF))

    def scatter_x(where_ref):
        wait(zr.at[seven], rs_r)
        for k in range(NREF):
            _, rz, rank = where_ref[k]
            for q in range(NX):
                yx[q, k] = zr[rz, rank, q]
        for d in (2, 1, 3):
            send(yx.at[at_x(d)], yr.at[x], y_s, y_r, dev_x(d))
        yr[x] = yx[x]

    half = NREF // 2
    halves = (pl.ds(0, half), pl.ds(half, half))

    def sign(way, d):
        return d if way == 0 else NZ - d

    def gather_first(h, where_ref):
        wait(yr.at[three], y_r)
        for k in range(NREF):
            rf[h][z, k] = yr[where_ref[k][0], k]
        for d in (2, 1):
            if d == 1:
                for way in range(2):
                    wait(rf[h].at[z], ag_s.at[h, way, 1])
            for way in range(2):
                send(
                    rf[h].at[z], rf[h].at[z], ag_s.at[h, way, d - 1], ag_r.at[h, way, d - 1], dev_z(sign(way, d))
                )

    def gather_second(h):
        for way in range(2):
            origin = at_z(sign(way, NZ - 2))
            wait(rf[h].at[origin], ag_r.at[h, way, 1])
            send(rf[h].at[origin], rf[h].at[origin], ag_s.at[h, way, 2], ag_r.at[h, way, 2], dev_z(sign(way, 1)))
            part = rf[h].at[origin, halves[way]]
            send(part, part, ag_s.at[h, way, 3], ag_r.at[h, way, 3], dev_z(sign(way, 2)))

    def gathered(h):
        for way in range(2):
            wait(rf[h].at[0], ag_r.at[h, way, 0])
            wait(rf[h].at[0], ag_r.at[h, way, 2])
            wait(rf[h].at[0, halves[way]], ag_r.at[h, way, 3])

    def solve():
        wait(da.at[seven], d2r.at[1])
        xt[...] = make_solver(da[...].reshape(NZ * NX * CAP, NACQ), ref_no)

    def facts_around():
        wait(info.at[three], ir)
        to_smem = pltpu.make_async_copy(info, info_s, i_sem)
        to_smem.start()
        wait(da.at[0, three], d2r.at[0])
        for d in range(1, NZ):
            send(da.at[z], da.at[z], d2s.at[1], d2r.at[1], dev_z(d))
        to_smem.wait()

    scatter_fill()
    pl.semaphore_wait(barrier, len(partners))
    scatter()
    for d in range(1, NX):
        send(info.at[x], info.at[x], is_, ir, dev_x(d))
        send(da.at[z, x], da.at[z, x], d2s.at[0], d2r.at[0], dev_x(d))
    for c in range(2):
        arrange(c)
        send_chunk(c, 0)
    for c in range(2, A_DEV):
        arrange(c)
    slots = lax.fori_loop(0, NACQ, find, (jnp.int32(0),) * NREF)
    slots = [jnp.minimum(slot, NACQ - 1) for slot in slots]
    owner = [lax.shift_right_logical(slot, 2) for slot in slots]
    where_ref = []
    for k in range(NREF):
        rank = jnp.int32(0)
        for other in range(NREF):
            if other != k:
                rank = rank + jnp.where((owner[other] == owner[k]) & (slots[other] < slots[k]), 1, 0)
        where_ref.append(
            (lax.shift_right_logical(owner[k], 3), lax.rem(owner[k], NZ), jnp.minimum(rank, chunks - 1))
        )
    scatter_x(where_ref)
    facts_around()
    wait(yx.at[three], y_s)
    for c in range(2, A_DEV):
        send_chunk(c, 0)
    gather_first(0, where_ref)
    gather_second(0)
    solve()

    def keep(q, v, columns):
        quant[q, :, columns] = v
        hlo[pl.ds(q, 1), columns] = v[0:1, :]
        hhi[pl.ds(q, 1), columns] = v[ROWS - 1 : ROWS, :]

    col = lax.broadcasted_iota(jnp.int32, (ROWS, COLS), 1)
    row = lax.broadcasted_iota(jnp.int32, (ROWS, COLS), 0)
    below = jnp.where(place > 0, 1.0, 0.0)
    above = jnp.where(place < 31, 1.0, 0.0)
    pairs_rows = 2 * CAP
    power_rows = pl.ds(2 * SLOTS, QPAD - 2 * SLOTS)

    def five(v):
        out = v
        for by in (1, 2):
            out = out + jnp.where(col >= by, pltpu.roll(v, by, 1), 0.0)
            out = out + jnp.where(col < COLS - by, pltpu.roll(v, COLS - by, 1), 0.0)
        return out

    def group_rows(group):
        return pl.ds(group * pairs_rows, pairs_rows)

    def send_halo(rows_, piece):
        send(hlo.at[rows_], rhi.at[rows_], h_s.at[0, piece], h_r.at[0, piece], dev_q(-1))
        send(hhi.at[rows_], rlo.at[rows_], h_s.at[1, piece], h_r.at[1, piece], dev_q(1))

    def halo_here(rows_, piece, count):
        wait(rhi.at[rows_], h_r.at[0, piece])
        wait(rlo.at[rows_], h_r.at[1, piece])
        for i in range(count // 8):
            block = pl.ds(rows_.start + 8 * i, 8)
            lo, hi = five(rlo[block, :]) * below, five(rhi[block, :]) * above
            rlo[block, :], rhi[block, :] = lo, hi

    def column_sums(start, count):
        def body(t, carry):
            values = [five(quant[start + 4 * t + i]) for i in range(4)]
            for i in range(4):
                quant[start + 4 * t + i] = values[i]
            return carry

        lax.fori_loop(0, count // 4, body, 0)

    def boxed(q):
        v = quant[q]
        down = jnp.where(row == 0, rlo[pl.ds(q, 1), :], pltpu.roll(v, 1, 0))
        up = jnp.where(row == ROWS - 1, rhi[pl.ds(q, 1), :], pltpu.roll(v, ROWS - 1, 0))
        return v + down + up

    for rest in (hlo, hhi):
        rest[QUANT:QPAD, :] = jnp.zeros((QPAD - QUANT, COLS), jnp.float32)
    gathered(0)
    for c in range(A_DEV):
        arrived(c, 0)
    full = pl.ds(0, COLS)
    for k in range(NREF):
        total = None
        for j in range(LOOKS):
            a, b = rf[0][j, k], rf[0][LOOKS + j, k]
            term = a * a + b * b
            total = term if j == 0 else total + term
        keep(2 * SLOTS + k, total, full)

    def power_body(s, carry):
        total = None
        for j in range(LOOKS):
            c, d = xg[0][lax.rem(s, A_DEV), s // A_DEV, 0, j], xg[0][lax.rem(s, A_DEV), s // A_DEV, 1, j]
            term = c * c + d * d
            total = term if j == 0 else total + term
        keep(2 * SLOTS + NREF + s, total, full)
        return carry

    def send_phases(part):
        here = pl.ds(pl.multiple_of(z * pairs_rows, pairs_rows), pairs_rows)
        for d in (4, 3, 5, 2, 6, 1, 7):
            block = pl.ds(pl.multiple_of(at_z(d) * pairs_rows, pairs_rows), pairs_rows)
            send(ph.at[part, :, block], pa.at[part, :, here], pa_s.at[part], pa_r.at[part], dev_z(d))
        pa[part, :, here] = ph[part, :, here]

    order_d = (2, 1, 3, 0)
    for group in range(NX):

        def slot_body(index, carry, group=group):
            kind, spot, live = info_s[group, index, 0], info_s[group, index, 1], info_s[group, index, 2]
            real = imag = None
            for j in range(LOOKS):
                a, b = rf[0][j, kind], rf[0][LOOKS + j, kind]
                c, e = xg[0][spot, group, 0, j], xg[0][spot, group, 1, j]
                re, im = a * c + b * e, b * c - a * e
                real, imag = (re, im) if j == 0 else (real + re, imag + im)
            keep(group * pairs_rows + index, real, full)
            keep(group * pairs_rows + CAP + index, imag, full)
            phase = jnp.where(live > 0, atan2(imag, real), 0.0)
            for b in range(BLOCKS):
                ph[group // 2, b, pl.ds(group % 2 * CAP + index, ROWS, stride=pairs_rows), :] = phase[
                    :, b * 128 : (b + 1) * 128
                ]
            return carry

        lax.fori_loop(0, CAP, slot_body, 0)
        send_halo(group_rows(group), group)
        if group % 2 == 1:
            send_phases(group // 2)

    lax.fori_loop(0, ACQS, power_body, 0)
    send_halo(power_rows, NX)
    column_sums(2 * SLOTS, NREF + ACQS)
    column_sums(at_x(order_d[0]) * pairs_rows, pairs_rows)
    halo_here(power_rows, NX, QPAD - 2 * SLOTS)

    def power_box(t, carry):
        values = [boxed(2 * SLOTS + 4 * t + i) for i in range(4)]
        for i in range(4):
            quant[2 * SLOTS + 4 * t + i] = values[i]
        return carry

    lax.fori_loop(0, (NREF + ACQS) // 4, power_box, 0)
    for group in range(NX):
        halo_here(group_rows(group), group, pairs_rows)
    quarter = pl.ds(pl.multiple_of(x * ROWS, ROWS), ROWS)
    for d in order_d:
        group = at_x(d)
        if d != order_d[0]:
            column_sums(group * pairs_rows, pairs_rows)

        def coherence_body(t, carry, group=group):
            values = []
            for i in range(2):
                index = 2 * t + i
                kind, spot, live = info_s[group, index, 0], info_s[group, index, 1], info_s[group, index, 2]
                real, imag = boxed(group * pairs_rows + index), boxed(group * pairs_rows + CAP + index)
                first = quant[2 * SLOTS + kind]
                second = quant[2 * SLOTS + NREF + group * A_DEV + spot]
                value = jnp.sqrt(real * real + imag * imag) / jnp.sqrt(first * second)
                values.append(jnp.where(live > 0, value, 0.0))
            for i in range(2):
                coh[group, 2 * t + i] = values[i]
            return carry

        lax.fori_loop(0, CAP // 2, coherence_body, 0)
        if d:
            send(coh.at[group], coherence.at[:, quarter, :], co_s, co_r, dev_x(d))
    coherence[:, quarter, :] = coh[x]

    arrivals = pl.ds(0, (NZ - 1) * pairs_rows)
    for part in range(2):
        wait(pa.at[part, :, arrivals], pa_r.at[part])
        weights = xt[...].reshape(NZ, SLOTS, NACQ)[:, part * pairs_rows : (part + 1) * pairs_rows]
        weights = weights.reshape(NZ * pairs_rows, NACQ)
        for b in range(BLOCKS):
            rows_b = pl.ds(b * 128, 128)
            term = dot(pa[part, b], weights, ((0,), (0,)))
            series[rows_b, :] = term if part == 0 else series[rows_b, :] + term

    wait(coh.at[three], co_r)
    wait(coh.at[three], co_s)
    wait(info.at[three], is_)
    wait(da.at[0, three], d2s.at[0])
    wait(da.at[seven], d2s.at[1])
    for h in range(nc):
        for c in range(A_DEV):
            sent(c, h)
        wait(zs.at[seven], rs_s)
        for part in range(2):
            wait(pa.at[part, :, arrivals], pa_s.at[part])
        for way in range(2):
            for step in (0, 2):
                wait(rf[h].at[0], ag_s.at[h, way, step])
            wait(rf[h].at[0, halves[way]], ag_s.at[h, way, 3])
        for way in range(2):
            wait(hlo.at[power_rows], h_s.at[way, NX])
            for group in range(NX):
                wait(hlo.at[pl.ds(0, pairs_rows)], h_s.at[way, group])


def call(chunks, nc, cid, stack, pairs, order, refs):
    width = COLS // nc
    f32 = jnp.float32
    dma = pltpu.SemaphoreType.DMA
    smem = pl.BlockSpec(memory_space=pltpu.SMEM)
    vmem = pl.BlockSpec(memory_space=pltpu.VMEM)
    return pl.pallas_call(
        functools.partial(kernel, chunks, nc),
        out_shape=(
            jax.ShapeDtypeStruct((COLS, NACQ), f32),
            jax.ShapeDtypeStruct((CAP, NX * ROWS, COLS), f32),
        ),
        in_specs=[pl.BlockSpec(memory_space=pl.ANY), smem, smem, smem],
        out_specs=(vmem, vmem),
        scratch_shapes=[
            pltpu.VMEM((A_DEV, BLOCKS, 2, NX * ROWS * LOOKS, 128), f32),
            pltpu.VMEM((A_DEV, NX, nc, 2, LOOKS, ROWS, width), f32),
            [pltpu.VMEM((A_DEV, NX, 2, LOOKS, ROWS, width), f32)] * nc,
            pltpu.VMEM((NZ, chunks, NX, ROWS, COLS), f32),
            pltpu.VMEM((NZ, chunks, NX, ROWS, COLS), f32),
            pltpu.VMEM((NX, NREF, ROWS, COLS), f32),
            pltpu.VMEM((NX, NREF, ROWS, COLS), f32),
            [pltpu.VMEM((NZ, NREF, ROWS, width), f32)] * nc,
            pltpu.VMEM((2, BLOCKS, ROWS * SLOTS // 2, 128), f32),
            pltpu.VMEM((2, BLOCKS, NZ * SLOTS // 2, 128), f32),
            pltpu.VMEM((NX, CAP, 128), jnp.int32),
            pltpu.SMEM((NX, CAP, 128), jnp.int32),
            pltpu.VMEM((NZ, NX, CAP, NACQ), f32),
            pltpu.VMEM((NZ * NX * CAP, NACQ), f32),
            pltpu.VMEM((QUANT, ROWS, COLS), f32),
            pltpu.VMEM((QPAD, COLS), f32),
            pltpu.VMEM((QPAD, COLS), f32),
            pltpu.VMEM((QPAD, COLS), f32),
            pltpu.VMEM((QPAD, COLS), f32),
            pltpu.VMEM((NX, CAP, ROWS, COLS), f32),
            dma((A_DEV, BLOCKS)), dma((A_DEV, nc)), dma((A_DEV, nc)), dma, dma, dma, dma((2,)), dma((2,)),
            dma, dma, dma, dma, dma((nc, 2, 4)), dma((nc, 2, 4)), dma((2,)), dma((2,)),
            dma((2, NX + 1)), dma((2, NX + 1)), dma, dma, dma((A_DEV, nc)),
        ],
        compiler_params=pltpu.CompilerParams(
            collective_id=cid, has_side_effects=True, vmem_limit_bytes=48 << 20
        ),
        name=f"sbas{chunks}",
    )(stack, pairs, order, refs)


def local(stack, pairs, order, refs):
    numbers = jnp.arange(NACQ, dtype=jnp.int32)
    slot = jnp.sum(jnp.where(order[None, :] == refs[:, None], numbers[None, :], 0), axis=1)
    owner = slot // A_DEV
    together = jnp.sum((owner[None, :] == owner[:, None]).astype(jnp.int32))
    pick = jnp.where(together > 8, 2, jnp.where(together > 4, 1, 0))
    variants = [functools.partial(call, 1, NC, 1), functools.partial(call, 2, NC, 2), functools.partial(call, 4, NC, 3)]
    return lax.switch(pick, variants, stack, pairs.T, order, refs)


NC = 1


def solution(mesh):
    return jax.shard_map(
        local,
        mesh=mesh,
        in_specs=(P("acq", None, "tile", None), P("acq", None), P(), P()),
        out_specs=(P(("tile", "acq"), None), P("acq", "tile", None)),
        check_vma=False,
    )
```
